256 devices in a mesh: slab: 16 (over z_lo, x, core), grp: 16 (over y, z_hi).
Axes of the slice: x: 4, y: 4, z: 8 (z_hi: 4, z_lo: 2; z = z_hi * 2 + z_lo), core: 2. Of those that a mesh axis runs over, the one named last changes fastest.
Arguments:
- vectors: bfloat16 [4096, 3072], P(('slab', 'grp')), may hold values from -6 to 6
- tiles: bfloat16 [32, 36864], replicated, may hold values from -0.09375 to 0.09375
- near_src: int32 [4096, 20], P(('slab', 'grp')), may hold values from 0 to 4095, as said below
- near_type: int32 [4096, 20], P(('slab', 'grp')), may hold values from 0 to 31, as said below
- near_count: int32 [4096], P(('slab', 'grp')), may hold values from 10 to 20
- bases: bfloat16 [4096, 6144], P(('slab', 'grp')), may hold values from -0.4375 to 0.4375
- far_src: int32 [4096, 32], P(('slab', 'grp')), may hold values from 0 to 4095, as said below
- coupling: bfloat16 [4096, 32, 1024], P(('slab', 'grp')), may hold values from -0.1875 to 0.1875
Outputs:
- first: bfloat16 [4096, 3072], P(('slab', 'grp'))
- second: bfloat16 [4096, 3072], P(('slab', 'grp'))
The draws below stay inside these ranges and needn't reach their ends.
Inputs may be any that keep to these rules, and one draw needn't show every extreme that they name: `near_src`: each source block is one of the same device's blocks, one of the last 8 blocks of the device with the same grp index in the previous slab, or one of the first 8 blocks of that device in the next slab; slabs are cyclic. `near_type`: the tile types of one block's slots are all different. `far_src`: each partner block lies in the same slab as the block.
All inputs are finite; a program needn't handle non-finite values.
Results may differ from the reference program's by a relative error of at most 0.0065.
Values may be sent and summed in bfloat16 or wider, within the bound.
No kernel may reach another device: no remote copies, remote signals or barrier semaphores. Data moves between devices by JAX's collectives and lax.ppermute only.
A program may use at most 64 MiB of HBM per device.

```python
import jax
import jax.numpy as jnp
from jax import lax

TILE = 192
RHS = 16
RANK = 32
TYPES = 32
NEAR = 20
FAR = 32
RIM = 8
B_DEV = 16
SLAB_BLOCKS = 256
BLOCKS = 4096


def draw_near_src(key, part):
    slab_count = BLOCKS // SLAB_BLOCKS
    blocks = jnp.arange(BLOCKS, dtype=jnp.int32)
    slab_of = blocks // SLAB_BLOCKS
    column_base = blocks % SLAB_BLOCKS // B_DEV * B_DEV
    kinds = jax.random.randint(jax.random.fold_in(key, 1), (BLOCKS, NEAR), 0, 5)
    own_pick = jax.random.randint(jax.random.fold_in(key, 2), (BLOCKS, NEAR), 0, B_DEV)
    rim_pick = jax.random.randint(jax.random.fold_in(key, 3), (BLOCKS, NEAR), 0, RIM)
    prev_slab = (slab_of - 1) % slab_count
    next_slab = (slab_of + 1) % slab_count
    own_block = (slab_of * SLAB_BLOCKS + column_base)[:, None] + own_pick
    prev_block = (prev_slab * SLAB_BLOCKS + column_base)[:, None] + (B_DEV - RIM) + rim_pick
    next_block = (next_slab * SLAB_BLOCKS + column_base)[:, None] + rim_pick
    chosen = jnp.where(kinds < 3, own_block, jnp.where(kinds == 3, prev_block, next_block))
    return chosen.astype(jnp.int32)


def draw_near_type(key, part):
    scores = jax.random.randint(jax.random.fold_in(key, 11), (BLOCKS, TYPES), 0, 1 << 20) * TYPES
    scores = scores + jnp.arange(TYPES, dtype=jnp.int32)[None, :]
    order = jnp.argsort(scores, axis=1, stable=True)
    return order[:, :NEAR].astype(jnp.int32)


def draw_near_count(key, part):
    counts = jax.random.randint(jax.random.fold_in(key, 21), (BLOCKS,), NEAR // 2, NEAR + 1)
    return counts.at[0].set(NEAR).astype(jnp.int32)


def draw_far_src(key, part):
    blocks = jnp.arange(BLOCKS, dtype=jnp.int32)
    slab_of = blocks // SLAB_BLOCKS
    picks = jax.random.randint(jax.random.fold_in(key, 31), (BLOCKS, FAR), 0, SLAB_BLOCKS)
    return (slab_of[:, None] * SLAB_BLOCKS + picks).astype(jnp.int32)


def block_levels(stream_key, extent, cuts, least, high):
    factor_of = 1.0
    for axis_at, parts in cuts:
        draws = jax.random.uniform(jax.random.fold_in(jax.random.fold_in(stream_key, 6), axis_at), (parts,), jnp.float32, least / len(cuts), high / len(cuts))
        factor_of = factor_of * jnp.repeat(jnp.exp(draws), extent[axis_at] // parts).reshape((-1,) + (1,) * (len(extent) - 1 - axis_at))
    return factor_of


def gaussian(rng, extent, spread, limit, pieces=(), kind=jnp.bfloat16):
    values = jax.random.normal(rng, extent, jnp.float32) * spread
    if len(pieces) > 0:
        values = block_levels(rng, extent, pieces, -0.22, 0.18) * values
    return jnp.clip(values, min=-limit, max=limit).astype(kind)


def setup_inputs(seed: int = 0) -> dict:
    streams_of = jax.random.split(jax.random.key(seed), 9)
    vectors = gaussian(streams_of[0], (BLOCKS, RHS * TILE), 1.0, 6.0, ((0, 256),))
    tiles = gaussian(streams_of[1], (TYPES, TILE * TILE), (TILE * NEAR) ** -0.5, 0.09375)
    near_src = draw_near_src(jax.random.fold_in(streams_of[8], 71), 0)
    near_type = draw_near_type(jax.random.fold_in(streams_of[8], 71), 0)
    near_count = draw_near_count(jax.random.fold_in(streams_of[8], 71), 0)
    bases = gaussian(streams_of[5], (BLOCKS, RANK * TILE), TILE ** -0.5, 0.4375, ((0, 256),))
    far_src = draw_far_src(jax.random.fold_in(streams_of[8], 71), 0)
    coupling = gaussian(streams_of[7], (BLOCKS, FAR, RANK * RANK), (RANK * FAR) ** -0.5, 0.1875, ((0, 256),))
    return dict(vectors=vectors, tiles=tiles, near_src=near_src, near_type=near_type, near_count=near_count, bases=bases, far_src=far_src, coupling=coupling)


def apply_operator(field, tiles, near_src, near_type, near_count, bases, far_src, coupling):
    block_count = field.shape[0]
    group_count = block_count // B_DEV
    highest = lax.Precision.HIGHEST
    coefficients = jnp.einsum('ipc,ihc->ihp', bases.astype(jnp.float32), field.astype(jnp.float32), precision=highest).astype(jnp.bfloat16)
    slot_ids = jnp.arange(NEAR, dtype=jnp.int32)

    def one_group(group_args):
        src_rows, type_rows, count_rows, basis_rows, partner_rows, coupling_rows = group_args
        sources = field[src_rows].astype(jnp.float32)
        chosen = tiles[type_rows].astype(jnp.float32)
        live_slot = (slot_ids[None, :] < count_rows[:, None]).astype(jnp.float32)
        near_term = jnp.einsum('ikdc,ikhc->ihd', chosen * live_slot[:, :, None, None], sources, precision=highest)
        partners = coefficients[partner_rows].astype(jnp.float32)
        couple = coupling_rows.astype(jnp.float32).reshape(B_DEV, FAR, RANK, RANK)
        far_mix = jnp.einsum('ikpq,ikhq->ihp', couple, partners, precision=highest).astype(jnp.bfloat16)
        far_term = jnp.einsum('ihp,ipc->ihc', far_mix.astype(jnp.float32), basis_rows.astype(jnp.float32), precision=highest)
        return (near_term + far_term).astype(jnp.bfloat16)

    grouped = (near_src.reshape(group_count, B_DEV, NEAR), near_type.reshape(group_count, B_DEV, NEAR),
               near_count.reshape(group_count, B_DEV), bases.reshape(group_count, B_DEV, RANK, TILE),
               far_src.reshape(group_count, B_DEV, FAR), coupling.reshape(group_count, B_DEV, FAR, RANK * RANK))
    result = lax.map(one_group, grouped)
    return result.reshape(block_count, RHS, TILE)


def reference(vectors, tiles, near_src, near_type, near_count, bases, far_src, coupling):
    field = vectors.reshape(BLOCKS, RHS, TILE)
    table = tiles.reshape(TYPES, TILE, TILE)
    basis = bases.reshape(BLOCKS, RANK, TILE)
    first = apply_operator(field, table, near_src, near_type, near_count, basis, far_src, coupling)
    second = apply_operator(first, table, near_src, near_type, near_count, basis, far_src, coupling)
    return (first.reshape(BLOCKS, RHS * TILE), second.reshape(BLOCKS, RHS * TILE))
```

```python
import functools

import jax
import jax.numpy as jnp
from jax import lax
from jax.experimental import pallas as pl
from jax.experimental.pallas import tpu as pltpu
from jax.sharding import PartitionSpec as P

TILE = 192
RHS = 16
RANK = 32
RIM = 8
LANES = 128
WIDE = 256
GROUP = 8

VMEM = pl.BlockSpec(memory_space=pltpu.VMEM)
SMEM = pl.BlockSpec(memory_space=pltpu.SMEM)
F32 = jnp.float32
BF16 = jnp.bfloat16
NT = (((1,), (1,)), ((), ()))
NN = (((1,), (0,)), ((), ()))


def params():
    return pltpu.CompilerParams(vmem_limit_bytes=40 * 1024 * 1024)


def project(field, basis_ref, blocks):
    rows, cols = GROUP * RHS, GROUP * RANK
    lane = lax.broadcasted_iota(jnp.int32, (RHS, LANES), 1) // RANK
    packed = []
    for g in range(blocks // GROUP):
        cross = lax.dot_general(
            field[g * rows : (g + 1) * rows, :],
            basis_ref[g * cols : (g + 1) * cols, :],
            NT,
            preferred_element_type=F32,
        )
        for half in range(GROUP // 4):
            out = None
            for j in range(4):
                at = (half * 4 + j) * RHS
                part = cross[at : at + RHS, half * LANES : (half + 1) * LANES]
                out = part if out is None else jnp.where(lane == j, part, out)
            packed.append(out)
    return jnp.concatenate(packed, axis=0).astype(BF16)


def halves(pair):
    low = lax.broadcasted_iota(jnp.int32, (pair.shape[0], LANES), 1) < LANES // 2
    one, two, three = (pair[:, j * LANES : (j + 1) * LANES] for j in range(3))
    two_turned, three_turned = (pltpu.roll(x, LANES // 2, 1) for x in (two, three))
    return (
        (one, jnp.where(low, two, 0.0)),
        (jnp.where(low, two_turned, three_turned), jnp.where(low, three_turned, 0.0)),
    )


def spread(source_ref, scratch, rows, count, stride):
    size = rows * stride
    for j in range(0, count, 2):
        pair = source_ref[:, j * TILE : (j + 2) * TILE].astype(F32)
        for k, parts in enumerate(halves(pair)):
            for side, part in enumerate(parts):
                scratch[pl.ds(side * size + j + k, rows, stride=stride), :] = part


def join(scratch, start, count, size):
    return jnp.concatenate(
        [scratch[side * size + start : side * size + start + count, :].astype(BF16) for side in range(2)],
        axis=1,
    )


def opening_kernel(v_ref, b_ref, lo_ref, hi_ref, basis_ref, coef_ref, f_s, b_s):
    blocks = v_ref.shape[0]
    rows, ranks = blocks * RHS, blocks * RANK
    spread(v_ref, f_s, blocks, RHS, RHS)
    spread(b_ref, b_s, blocks, RANK, RANK)
    field = join(f_s, 0, rows, rows)
    rim = RIM * RHS
    lo_ref[...] = field[:rim]
    hi_ref[...] = field[rim:]
    basis_ref[...] = join(b_s, 0, ranks, ranks)
    packed = project(field, basis_ref, blocks)
    for j in range(coef_ref.shape[0]):
        coef_ref[j] = packed


def layout_kernel(
    slab_blocks, tiles_ref, coup_ref, far_ref, table_ref, mat_ref, idx_ref, t_s, c_s, m_s
):
    types = tiles_ref.shape[0]
    blocks, partners, _ = coup_ref.shape
    spread(tiles_ref, t_s, types, TILE, TILE)
    for t in range(types):
        table_ref[t] = join(t_s, t * TILE, TILE, types * TILE)

    deep = partners // 4
    rows = blocks * RANK
    lane = lax.broadcasted_iota(jnp.int32, (deep, LANES), 1) // RANK

    def one_block(i, _):
        for big in range(RANK // 4):
            at = big * partners
            c_s[at : at + partners, :] = coup_ref[i, :, big * LANES : (big + 1) * LANES].astype(F32)
        for big in range(RANK // 4):
            parts = [
                c_s[pl.ds(big * partners + j, deep, stride=4), :] for j in range(4)
            ]
            turned = [
                [parts[j] if r == 0 else pltpu.roll(parts[j], r * RANK, 1) for r in range(4)]
                for j in range(4)
            ]
            for small in range(4):
                out = turned[0][(0 - small) % 4]
                for j in range(1, 4):
                    out = jnp.where(lane == j, turned[j][(j - small) % 4], out)
                m_s[pl.ds(i * RANK + big * 4 + small, deep, stride=rows), :] = out
        return 0

    lax.fori_loop(0, blocks, one_block, 0)
    for k in range(deep):
        mat_ref[:, k * LANES : (k + 1) * LANES] = m_s[k * rows : (k + 1) * rows, :].astype(BF16)

    source = far_ref[...] % slab_blocks
    slot = lax.broadcasted_iota(jnp.int32, source.shape, 1)
    idx_ref[...] = ((slot - source) & 3) * (slab_blocks // 4) + source // 4


def near_kernel(
    slabs, slab_blocks,
    me_ref, src_ref, type_ref, count_ref, lo_ref, hi_ref, prev_ref, next_ref, table_ref,
    out_ref, e_s, p_s,
):
    blocks, slots = src_ref.shape
    types = table_ref.shape[0]
    rim = RIM * RHS
    e_s[0:rim, :] = lo_ref[...]
    e_s[rim : 2 * rim, :] = hi_ref[...]
    e_s[2 * rim : 3 * rim, :] = prev_ref[...]
    e_s[3 * rim : 4 * rim, :] = next_ref[...]
    p_s[0:types] = jnp.zeros((types,) + p_s.shape[1:], BF16)
    me = me_ref[0]

    def one_block(i, _):
        count = count_ref[i]
        for k in range(slots):
            source = src_ref[i, k]
            step = lax.rem(source // slab_blocks - me + slabs, slabs)
            local = lax.rem(source, blocks)
            at = local + jnp.where(step == 0, 0, jnp.where(step == 1, 3 * RIM, RIM))
            kind = jnp.where(k < count, type_ref[i, k], types)
            slab = e_s[pl.ds(pl.multiple_of(at * RHS, RHS), RHS), :]
            p_s[kind, pl.ds(pl.multiple_of(i * RHS, RHS), RHS), :] = slab
        return 0

    lax.fori_loop(0, blocks, one_block, 0)
    half = blocks * RHS // 2
    for a in range(2):
        total = None
        for t in range(types):
            term = lax.dot_general(
                p_s[t, a * half : (a + 1) * half, :], table_ref[t], NT, preferred_element_type=F32
            )
            total = term if total is None else total + term
        out_ref[a * half : (a + 1) * half, LANES:] = jnp.zeros((half, LANES), F32)
        out_ref[a * half : (a + 1) * half, :TILE] = total


def far_kernel(last, idx_ref, got_ref, mat_ref, basis_ref, near_ref, *rest):
    if last:
        y_ref, turn_s, pick_s, sum_s = rest
    else:
        y_ref, lo_ref, hi_ref, coef_ref, turn_s, pick_s, sum_s = rest
    blocks, partners = idx_ref.shape
    peers, packed_rows, _ = got_ref.shape
    quarter = peers * packed_rows
    for j in range(peers):
        got = got_ref[j].astype(F32)
        for r in range(4):
            turned = got if r == 0 else pltpu.roll(got, r * RANK, 1)
            at = r * quarter + j * packed_rows
            turn_s[at : at + packed_rows, :] = turned.astype(BF16)
    lane = lax.broadcasted_iota(jnp.int32, (RHS, LANES), 1) // RANK

    def one_block(i, _):
        for k in range(partners // 4):
            out = None
            for j in range(4):
                at = pl.multiple_of(idx_ref[i, k * 4 + j] * RHS, RHS)
                part = turn_s[pl.ds(at, RHS), :]
                out = part if out is None else jnp.where(lane == j, part, out)
            pick_s[pl.ds(pl.multiple_of(i * RHS, RHS), RHS), k * LANES : (k + 1) * LANES] = out
        return 0

    lax.fori_loop(0, blocks, one_block, 0)
    size = blocks * RHS
    rows, cols = GROUP * RHS, GROUP * RANK
    own = (
        lax.broadcasted_iota(jnp.int32, (rows, cols), 0) // RHS
        == lax.broadcasted_iota(jnp.int32, (rows, cols), 1) // RANK
    )
    for g in range(blocks // GROUP):
        cross = lax.dot_general(
            pick_s[g * rows : (g + 1) * rows, :],
            mat_ref[g * cols : (g + 1) * cols, :],
            NT,
            preferred_element_type=F32,
        )
        mix = jnp.where(own, cross, 0.0).astype(BF16)
        far = lax.dot_general(
            mix, basis_ref[g * cols : (g + 1) * cols, :], NN, preferred_element_type=F32
        )
        total = near_ref[g * rows : (g + 1) * rows, :] + far
        sum_s[g * rows : (g + 1) * rows, :] = total[:, :LANES]
        sum_s[size + g * rows : size + (g + 1) * rows, :] = total[:, LANES:]
    if not last:
        field = join(sum_s, 0, size, size)
        rim = RIM * RHS
        lo_ref[...] = field[:rim]
        hi_ref[...] = field[rim:]
        packed = project(field, basis_ref, blocks)
        for j in range(coef_ref.shape[0]):
            coef_ref[j] = packed
    low = lax.broadcasted_iota(jnp.int32, (blocks, LANES), 1) < LANES // 2
    for h in range(0, RHS, 2):
        one, two, three, four = (
            sum_s[pl.ds(side * size + h + k, blocks, stride=RHS), :]
            for k in range(2)
            for side in range(2)
        )
        three, four = (pltpu.roll(x, LANES // 2, 1) for x in (three, four))
        pair = (one, jnp.where(low, two, three), jnp.where(low, three, four))
        for j in range(3):
            at = h * TILE + j * LANES
            y_ref[:, at : at + LANES] = pair[j].astype(BF16)


def per_device(vectors, tiles, near_src, near_type, near_count, bases, far_src, coupling):
    blocks = vectors.shape[0]
    types = tiles.shape[0]
    partners = far_src.shape[1]
    slabs, peers = lax.axis_size("slab"), lax.axis_size("grp")
    slab_blocks = blocks * peers
    rows = blocks * RHS
    rim = RIM * RHS
    ranks = blocks * RANK
    packed = rows // 4
    shape = jax.ShapeDtypeStruct
    up = [(i, (i + 1) % slabs) for i in range(slabs)]
    down = [(j, i) for i, j in up]
    me = lax.axis_index("slab").astype(jnp.int32).reshape(1)

    lo, hi, basis, coef = pl.pallas_call(
        opening_kernel,
        out_shape=(
            shape((rim, WIDE), BF16),
            shape((rim, WIDE), BF16),
            shape((ranks, WIDE), BF16),
            shape((peers, packed, LANES), BF16),
        ),
        in_specs=[VMEM] * 2,
        out_specs=(VMEM,) * 4,
        scratch_shapes=[pltpu.VMEM((2 * rows, LANES), F32), pltpu.VMEM((2 * ranks, LANES), F32)],
        compiler_params=params(),
        name="opening",
    )(vectors, bases)

    table, mat, idx = pl.pallas_call(
        functools.partial(layout_kernel, slab_blocks),
        out_shape=(
            shape((types, TILE, WIDE), BF16),
            shape((ranks, partners * RANK), BF16),
            shape(far_src.shape, jnp.int32),
        ),
        in_specs=[VMEM] * 3,
        out_specs=(VMEM,) * 3,
        scratch_shapes=[
            pltpu.VMEM((2 * types * TILE, LANES), F32),
            pltpu.VMEM((partners * RANK // 4, LANES), F32),
            pltpu.VMEM((partners // 4 * ranks, LANES), F32),
        ],
        compiler_params=params(),
        cost_estimate=pl.CostEstimate(flops=0, bytes_accessed=12_000_000, transcendentals=0),
        name="layout",
    )(tiles, coupling, far_src)

    def near(lo, hi):
        prev = lax.ppermute(hi, "slab", up)
        succ = lax.ppermute(lo, "slab", down)
        return pl.pallas_call(
            functools.partial(near_kernel, slabs, slab_blocks),
            out_shape=shape((rows, WIDE), F32),
            in_specs=[SMEM] * 4 + [VMEM] * 5,
            out_specs=VMEM,
            scratch_shapes=[
                pltpu.VMEM((4 * rim, WIDE), BF16),
                pltpu.VMEM((types + 1, rows, WIDE), BF16),
            ],
            compiler_params=params(),
            cost_estimate=pl.CostEstimate(flops=0, bytes_accessed=12_000_000, transcendentals=0),
            name="near",
        )(me, near_src, near_type, near_count, lo, hi, prev, succ, table)

    def far(last, got, near_term):
        field = [shape((blocks, RHS * TILE), BF16)]
        if not last:
            field += [
                shape((rim, WIDE), BF16),
                shape((rim, WIDE), BF16),
                shape((peers, packed, LANES), BF16),
            ]
        return pl.pallas_call(
            functools.partial(far_kernel, last),
            out_shape=tuple(field),
            in_specs=[SMEM] + [VMEM] * 4,
            out_specs=(VMEM,) * len(field),
            scratch_shapes=[
                pltpu.VMEM((4 * peers * packed, LANES), BF16),
                pltpu.VMEM((rows, partners * RANK), BF16),
                pltpu.VMEM((2 * rows, LANES), F32),
            ],
            compiler_params=params(),
            name="far_last" if last else "far_first",
        )(idx, got, mat, basis, near_term)

    got = lax.all_to_all(coef, "grp", 0, 0, tiled=True)
    near_term = near(lo, hi)
    first, lo, hi, coef = far(False, got, near_term)
    got = lax.all_to_all(coef, "grp", 0, 0, tiled=True)
    near_term = near(lo, hi)
    (second,) = far(True, got, near_term)
    return (first, second)


def solution(mesh):
    in_specs = (
        P(("slab", "grp"), None),
        P(),
        P(("slab", "grp"), None),
        P(("slab", "grp"), None),
        P(("slab", "grp")),
        P(("slab", "grp"), None),
        P(("slab", "grp"), None),
        P(("slab", "grp"), None, None),
    )
    out_specs = (P(("slab", "grp"), None), P(("slab", "grp"), None))
    return jax.shard_map(
        per_device, mesh=mesh, in_specs=in_specs, out_specs=out_specs, check_vma=False
    )
```

```python
import functools

import jax
import jax.numpy as jnp
from jax import lax
from jax.experimental import pallas as pl
from jax.experimental.pallas import tpu as pltpu
from jax.sharding import PartitionSpec as P

TILE = 192
RHS = 16
RANK = 32
RIM = 8
LANES = 128
WIDE = 256
GROUP = 8
SIDE = LANES // RANK

VMEM = pl.BlockSpec(memory_space=pltpu.VMEM)
SMEM = pl.BlockSpec(memory_space=pltpu.SMEM)
HBM = pl.BlockSpec(memory_space=pltpu.HBM)
F32 = jnp.float32
BF16 = jnp.bfloat16
NT = (((1,), (1,)), ((), ()))
NN = (((1,), (0,)), ((), ()))
shape = jax.ShapeDtypeStruct


def call(kernel, name, args, ins, outs, scratch, mib, moved=0):
    args = [
        pltpu.with_memory_space_constraint(a, pltpu.HBM) if s is HBM else a
        for a, s in zip(args, ins)
    ]
    return pl.pallas_call(
        kernel,
        out_shape=tuple(o for o, _ in outs),
        in_specs=ins,
        out_specs=tuple(s for _, s in outs),
        scratch_shapes=scratch,
        compiler_params=pltpu.CompilerParams(vmem_limit_bytes=mib * 1024 * 1024),
        cost_estimate=pl.CostEstimate(flops=0, bytes_accessed=moved, transcendentals=0),
        name=name,
    )(*args)


def iota(shape, axis):
    return lax.broadcasted_iota(jnp.int32, shape, axis)


def swap(rows, outer):
    at = iota((rows, rows), 0)
    source = (at % outer) * (rows // outer) + at // outer
    return (iota((rows, rows), 1) == source).astype(BF16)


def turn(x):
    return pltpu.roll(x, LANES // 2, 1)


def halves(pair):
    low = iota((pair.shape[0], LANES), 1) < LANES // 2
    one, two, three = (pair[:, j * LANES : (j + 1) * LANES] for j in range(3))
    two_turned, three_turned = turn(two), turn(three)
    zero = jnp.zeros_like(two)
    return (
        (one, jnp.where(low, two, zero)),
        (jnp.where(low, two_turned, three_turned), jnp.where(low, three_turned, zero)),
    )


def spread(source_ref, scratch, rows, count):
    size = rows * count
    for j in range(0, count, 2):
        pair = source_ref[:, j * TILE : (j + 2) * TILE].astype(F32)
        for k, parts in enumerate(halves(pair)):
            for side, part in enumerate(parts):
                scratch[pl.ds(side * size + j + k, rows, stride=count), :] = part


def gather_sides(scratch, y_ref, blocks):
    size = blocks * RHS
    low = iota((blocks, LANES), 1) < LANES // 2
    for h in range(0, RHS, 2):
        one, two, three, four = (
            scratch[pl.ds(side * size + h + k, blocks, stride=RHS), :]
            for k in range(2)
            for side in range(2)
        )
        three, four = turn(three), turn(four)
        pair = (one, jnp.where(low, two, three), jnp.where(low, three, four))
        for j in range(3):
            at = h * TILE + j * LANES
            y_ref[:, at : at + LANES] = pair[j].astype(BF16)


def join(scratch, size):
    return jnp.concatenate(
        [scratch[side * size : (side + 1) * size, :].astype(BF16) for side in range(2)], axis=1
    )


def opening_kernel(v_hbm, b_hbm, lo_ref, hi_ref, basis_ref, v_s, b_s, f_s, g_s, sems):
    blocks = v_s.shape[0]
    rows, ranks = blocks * RHS, blocks * RANK
    get_v = pltpu.make_async_copy(v_hbm, v_s, sems.at[0])
    get_b = pltpu.make_async_copy(b_hbm, b_s, sems.at[1])
    get_v.start()
    get_b.start()
    get_v.wait()
    spread(v_s, f_s, blocks, RHS)
    field = join(f_s, rows)
    rim = RIM * RHS
    lo_ref[...] = field[:rim]
    hi_ref[...] = field[rim:]
    get_b.wait()
    spread(b_s, g_s, blocks, RANK)
    basis_ref[...] = join(g_s, ranks)


def project_kernel(lo_ref, hi_ref, basis_ref, coef_hbm, coef_s, sem):
    rows, cols = GROUP * RHS, GROUP * RANK
    lane = iota((RHS, LANES), 1) // RANK
    for g, field_ref in enumerate((lo_ref, hi_ref)):
        cross = lax.dot_general(
            field_ref[...],
            basis_ref[g * cols : (g + 1) * cols, :],
            NT,
            preferred_element_type=F32,
        )
        for half in range(GROUP // SIDE):
            out = None
            for j in range(SIDE):
                at = (half * SIDE + j) * RHS
                part = cross[at : at + RHS, half * LANES : (half + 1) * LANES]
                out = part if out is None else jnp.where(lane == j, part, out)
            at = (g * (GROUP // SIDE) + half) * RHS
            for j in range(coef_s.shape[0]):
                coef_s[j, at : at + RHS, :] = out.astype(BF16)
    put = pltpu.make_async_copy(coef_s, coef_hbm, sem)
    put.start()
    put.wait()


def layout_kernel(
    slabs, slab_blocks,
    me_ref, count_ref, src_hbm, type_hbm, far_hbm, tiles_hbm, coup_hbm,
    table_ref, mat_ref, far_idx_ref, at_ref, kind_ref,
    src_s, type_s, far_s, tiles_s, coup_s, sems,
):
    gets = [
        pltpu.make_async_copy(source, to, sems.at[j])
        for j, (source, to) in enumerate(
            (
                (coup_hbm, coup_s),
                (src_hbm, src_s),
                (type_hbm, type_s),
                (far_hbm, far_s),
                (tiles_hbm, tiles_s),
            )
        )
    ]
    for get in gets:
        get.start()
    types = tiles_s.shape[0]
    blocks, partners, _ = coup_s.shape
    deep = partners // SIDE

    lane = iota((deep, LANES), 1) // RANK
    order = swap(RANK * deep, RANK)
    gets[0].wait()

    def two_blocks(n, _):
        stacks = []
        for b in range(2):
            i = 2 * n + b
            stack = []
            for big in range(RANK // SIDE):
                x = coup_s[i, :, big * LANES : (big + 1) * LANES].astype(F32)
                parts = [x[j * deep : (j + 1) * deep] for j in range(SIDE)]
                turned = [
                    [p if r == 0 else pltpu.roll(p, r * RANK, 1) for r in range(SIDE)]
                    for p in parts
                ]
                for small in range(SIDE):
                    out = turned[0][-small % SIDE]
                    for j in range(1, SIDE):
                        out = jnp.where(lane == j, turned[j][(j - small) % SIDE], out)
                    stack.append(out)
            stacks.append(jnp.concatenate(stack, axis=0).astype(BF16))
        both = jnp.concatenate(stacks, axis=1)
        both = lax.dot_general(order, both, NN, preferred_element_type=F32).astype(BF16)
        for b in range(2):
            at = pl.multiple_of((2 * n + b) * RANK, RANK)
            for k in range(deep):
                part = both[k * RANK : (k + 1) * RANK, b * LANES : (b + 1) * LANES]
                mat_ref[pl.ds(at, RANK), k * LANES : (k + 1) * LANES] = part
        return 0

    lax.fori_loop(0, blocks // 2, two_blocks, 0, unroll=True)

    many = 16
    order = swap(many * many, many)
    for get in gets[1:4]:
        get.wait()
    source = far_s[...] % slab_blocks
    group = iota(source.shape, 1) // deep
    turned = (group - source) & (SIDE - 1)
    far_idx_ref[...] = (turned * (slab_blocks // SIDE) + source // SIDE) * RHS

    source = src_s[...]
    step = (source // slab_blocks - me_ref[0] + slabs) % slabs
    offset = jnp.where(step == 0, 0, jnp.where(step == 1, 3 * RIM, RIM))
    at_ref[...] = (source % blocks + offset) * RHS
    row = iota(source.shape, 0)
    count = jnp.zeros(source.shape, jnp.int32)
    for i in range(blocks):
        count = jnp.where(row == i, count_ref[i], count)
    kind_ref[...] = jnp.where(iota(source.shape, 1) < count, type_s[...], types) * WIDE

    gets[4].wait()

    def some_rows(n, _):
        at = pl.multiple_of(n * many * TILE, many * TILE)
        for a in range(types // many):
            stack = []
            for d in range(0, many, 2):
                pair = tiles_s[a * many : (a + 1) * many, pl.ds(at + d * TILE, 2 * TILE)]
                stack += [jnp.concatenate(parts, axis=1) for parts in halves(pair)]
            out = jnp.concatenate(stack, axis=0)
            out = lax.dot_general(order, out, NN, preferred_element_type=F32).astype(BF16)
            for t in range(many):
                to = (a * many + t) * WIDE
                table_ref[pl.ds(pl.multiple_of(n * many, many), many), to : to + WIDE] = out[
                    t * many : (t + 1) * many
                ]
        return 0

    lax.fori_loop(0, TILE // many, some_rows, 0, unroll=True)


def near_kernel(
    give, at_ref, kind_ref, lo_ref, hi_ref, prev_ref, next_ref, table_ref, out_ref, *rest
):
    if give:
        y_ref, e_s, p_s, f_s = rest
    else:
        e_s, p_s = rest
    blocks, slots = at_ref.shape
    size = blocks * RHS
    rim = RIM * RHS
    for j, ref in enumerate((lo_ref, hi_ref, prev_ref, next_ref)):
        e_s[j * rim : (j + 1) * rim, :] = ref[...]
    columns = table_ref.shape[1]
    p_s[:, :columns] = jnp.zeros((size, columns), BF16)

    def one_block(i, _):
        row = pl.multiple_of(i * RHS, RHS)
        for k in range(slots):
            source = pl.multiple_of(at_ref[i, k], RHS)
            column = pl.multiple_of(kind_ref[i, k], WIDE)
            p_s[pl.ds(row, RHS), pl.ds(column, WIDE)] = e_s[pl.ds(source, RHS), :]
        return 0

    lax.fori_loop(0, blocks, one_block, 0, unroll=True)
    if give:
        for j in range(2):
            f_s[j * size : (j + 1) * size, :] = e_s[:size, j * LANES : (j + 1) * LANES].astype(F32)
        gather_sides(f_s, y_ref, blocks)
    out_ref[:, LANES:] = jnp.zeros((size, LANES), F32)
    out_ref[:, :TILE] = lax.dot_general(
        p_s[:, :columns], table_ref[...], NT, preferred_element_type=F32
    )


def far_kernel(last, idx_ref, got_ref, mat_ref, basis_ref, near_ref, *rest):
    if last:
        y_ref, turn_s, pick_s, sum_s = rest
    else:
        lo_ref, hi_ref, turn_s, pick_s = rest
    blocks, partners = idx_ref.shape
    deep = partners // SIDE
    peers, packed_rows, _ = got_ref.shape
    quarter = peers * packed_rows
    for j in range(peers):
        got = got_ref[j]
        for r in range(SIDE):
            at = r * quarter + j * packed_rows
            turn_s[at : at + packed_rows, :] = got if r == 0 else pltpu.roll(got, r * RANK, 1)
    lane = iota((RHS, LANES), 1) // RANK

    def one_block(i, _):
        row = pl.multiple_of(i * RHS, RHS)
        for k in range(deep):
            out = None
            for j in range(SIDE):
                at = pl.multiple_of(idx_ref[i, j * deep + k], RHS)
                part = turn_s[pl.ds(at, RHS), :]
                out = part if out is None else jnp.where(lane == j, part, out)
            pick_s[pl.ds(row, RHS), k * LANES : (k + 1) * LANES] = out
        return 0

    lax.fori_loop(0, blocks, one_block, 0, unroll=True)
    size = blocks * RHS
    rows, cols = GROUP * RHS, GROUP * RANK
    own = iota((rows, cols), 0) // RHS == iota((rows, cols), 1) // RANK
    for g in range(blocks // GROUP):
        cross = lax.dot_general(
            pick_s[g * rows : (g + 1) * rows, :],
            mat_ref[g * cols : (g + 1) * cols, :],
            NT,
            preferred_element_type=F32,
        )
        mix = jnp.where(own, cross, 0.0).astype(BF16)
        far = lax.dot_general(
            mix, basis_ref[g * cols : (g + 1) * cols, :], NN, preferred_element_type=F32
        )
        total = near_ref[g * rows : (g + 1) * rows, :] + far
        if last:
            for j in range(2):
                at = j * size + g * rows
                sum_s[at : at + rows, :] = total[:, j * LANES : (j + 1) * LANES]
        else:
            (lo_ref, hi_ref)[g][...] = total.astype(BF16)
    if last:
        gather_sides(sum_s, y_ref, blocks)


def opening(vectors, bases):
    blocks = vectors.shape[0]
    rows, ranks, rim = blocks * RHS, blocks * RANK, RIM * RHS
    field = (shape((rim, WIDE), BF16), VMEM)
    return call(
        opening_kernel, "opening", (vectors, bases), [HBM] * 2,
        [field, field, (shape((ranks, WIDE), BF16), VMEM)],
        [
            pltpu.VMEM(vectors.shape, BF16),
            pltpu.VMEM(bases.shape, BF16),
            pltpu.VMEM((2 * rows, LANES), F32),
            pltpu.VMEM((2 * ranks, LANES), F32),
            pltpu.SemaphoreType.DMA((2,)),
        ],
        8,
    )


def project(peers, lo, hi, basis):
    packed = lo.shape[0] * 2 // SIDE
    coef = (peers, packed, LANES)
    return call(
        project_kernel, "project", (lo, hi, basis), [VMEM] * 3,
        [(shape(coef, BF16), HBM)],
        [pltpu.VMEM(coef, BF16), pltpu.SemaphoreType.DMA],
        4,
    )[0]


def layout(slabs, peers, me, near_count, near_src, near_type, far_src, tiles, coupling):
    blocks, partners, _ = coupling.shape
    types = tiles.shape[0]
    table = (TILE, types * WIDE)
    slots = shape(near_src.shape, jnp.int32)
    return call(
        functools.partial(layout_kernel, slabs, blocks * peers), "layout",
        (me, near_count, near_src, near_type, far_src, tiles, coupling),
        [SMEM] * 2 + [HBM] * 5,
        [
            (shape(table, BF16), VMEM),
            (shape((blocks * RANK, partners * RANK), BF16), VMEM),
            (shape(far_src.shape, jnp.int32), VMEM),
            (slots, VMEM),
            (slots, VMEM),
        ],
        [
            pltpu.VMEM(near_src.shape, jnp.int32),
            pltpu.VMEM(near_src.shape, jnp.int32),
            pltpu.VMEM(far_src.shape, jnp.int32),
            pltpu.VMEM(tiles.shape, BF16),
            pltpu.VMEM(coupling.shape, BF16),
            pltpu.SemaphoreType.DMA((5,)),
        ],
        16, 12_000_000,
    )


def near(give, at, kind, lo, hi, prev, succ, table):
    rim = lo.shape[0]
    rows = 2 * rim
    outs = [(shape((rows, WIDE), F32), VMEM)]
    scratch = [
        pltpu.VMEM((2 * rows, WIDE), BF16),
        pltpu.VMEM((rows, table.shape[1] + WIDE), BF16),
    ]
    if give:
        outs.append((shape((rows // RHS, RHS * TILE), BF16), VMEM))
        scratch.append(pltpu.VMEM((2 * rows, LANES), F32))
    return call(
        functools.partial(near_kernel, give), "near_give" if give else "near",
        (at, kind, lo, hi, prev, succ, table),
        [SMEM] * 2 + [VMEM] * 5, outs, scratch, 16, 12_000_000,
    )


def far(last, idx, got, mat, basis, near_term):
    rows = near_term.shape[0]
    peers, packed, _ = got.shape
    scratch = [
        pltpu.VMEM((SIDE * peers * packed, LANES), BF16),
        pltpu.VMEM((rows, mat.shape[1]), BF16),
    ]
    if last:
        outs = [(shape((rows // RHS, RHS * TILE), BF16), VMEM)]
        scratch.append(pltpu.VMEM((2 * rows, LANES), F32))
    else:
        outs = [(shape((rows // 2, WIDE), BF16), VMEM)] * 2
    return call(
        functools.partial(far_kernel, last), "far_last" if last else "far",
        (idx, got, mat, basis, near_term), [SMEM] + [VMEM] * 4, outs, scratch, 8,
    )


def per_device(vectors, tiles, near_src, near_type, near_count, bases, far_src, coupling):
    slabs, peers = lax.axis_size("slab"), lax.axis_size("grp")
    up = [(i, (i + 1) % slabs) for i in range(slabs)]
    down = [(j, i) for i, j in up]
    me = lax.axis_index("slab").astype(jnp.int32).reshape(1)

    def halo(lo, hi):
        return lax.ppermute(hi, "slab", up), lax.ppermute(lo, "slab", down)

    def exchange(lo, hi, basis):
        return lax.all_to_all(project(peers, lo, hi, basis), "grp", 0, 0, tiled=True)

    lo, hi, basis = opening(vectors, bases)
    prev, succ = halo(lo, hi)
    got = exchange(lo, hi, basis)
    table, mat, idx, at, kind = layout(
        slabs, peers, me, near_count, near_src, near_type, far_src, tiles, coupling
    )
    (near_term,) = near(False, at, kind, lo, hi, prev, succ, table)
    lo, hi = far(False, idx, got, mat, basis, near_term)
    prev, succ = halo(lo, hi)
    got = exchange(lo, hi, basis)
    near_term, first = near(True, at, kind, lo, hi, prev, succ, table)
    (second,) = far(True, idx, got, mat, basis, near_term)
    return (first, second)


def solution(mesh):
    in_specs = (
        P(("slab", "grp"), None),
        P(),
        P(("slab", "grp"), None),
        P(("slab", "grp"), None),
        P(("slab", "grp")),
        P(("slab", "grp"), None),
        P(("slab", "grp"), None),
        P(("slab", "grp"), None, None),
    )
    out_specs = (P(("slab", "grp"), None), P(("slab", "grp"), None))
    return jax.shard_map(
        per_device, mesh=mesh, in_specs=in_specs, out_specs=out_specs, check_vma=False
    )
```

```python
import functools

import jax
import jax.numpy as jnp
from jax import lax
from jax.experimental import pallas as pl
from jax.experimental.pallas import tpu as pltpu
from jax.sharding import PartitionSpec as P

TILE = 192
RHS = 16
RANK = 32
RIM = 8
LANES = 128
WIDE = 256
GROUP = 8
LONG = 1_000_000_000_000
STEPS = 2
SIDE = LANES // RANK

VMEM = pl.BlockSpec(memory_space=pltpu.VMEM)
SMEM = pl.BlockSpec(memory_space=pltpu.SMEM)
HBM = pl.BlockSpec(memory_space=pltpu.HBM)
ANY = pl.BlockSpec(memory_space=pl.ANY)
F32 = jnp.float32
BF16 = jnp.bfloat16
NT = (((1,), (1,)), ((), ()))
NN = (((1,), (0,)), ((), ()))
shape = jax.ShapeDtypeStruct


def call(kernel, name, args, ins, outs, scratch, mib, moved=0):
    args = [
        pltpu.with_memory_space_constraint(a, pltpu.HBM) if s is HBM else a
        for a, s in zip(args, ins)
    ]
    return pl.pallas_call(
        kernel,
        out_shape=tuple(pltpu.HBM(o.shape, o.dtype) if s is HBM else o for o, s in outs),
        in_specs=ins,
        out_specs=tuple(s for _, s in outs),
        scratch_shapes=scratch,
        compiler_params=pltpu.CompilerParams(vmem_limit_bytes=mib * 1024 * 1024),
        cost_estimate=pl.CostEstimate(flops=100 * moved, bytes_accessed=moved, transcendentals=0),
        name=name,
    )(*args)


def copies(pairs, sems, first=0):
    return [
        pltpu.make_async_copy(source, to, sems.at[first + j]) for j, (source, to) in enumerate(pairs)
    ]


def start(group):
    for copy in group:
        copy.start()


def wait(group):
    for copy in group:
        copy.wait()


def iota(shape, axis):
    return lax.broadcasted_iota(jnp.int32, shape, axis)


def swap(rows, outer):
    at = iota((rows, rows), 0)
    source = (at % outer) * (rows // outer) + at // outer
    return (iota((rows, rows), 1) == source).astype(BF16)


def turn(x):
    return pltpu.roll(x, LANES // 2, 1)


def halves(pair):
    low = iota((pair.shape[0], LANES), 1) < LANES // 2
    one, two, three = (pair[:, j * LANES : (j + 1) * LANES] for j in range(3))
    two_turned, three_turned = turn(two), turn(three)
    zero = jnp.zeros_like(two)
    return (
        (one, jnp.where(low, two, zero)),
        (jnp.where(low, two_turned, three_turned), jnp.where(low, three_turned, zero)),
    )


def spread(source_ref, scratch, rows, count, late=None):
    size = rows * count
    for j in range(0, count, 2):
        pair = source_ref[:, j * TILE : (j + 2) * TILE].astype(F32)
        if late is not None:
            pair = jnp.where(late, pair[rows:], pair[:rows])
        for k, parts in enumerate(halves(pair)):
            for side, part in enumerate(parts):
                scratch[pl.ds(side * size + j + k, rows, stride=count), :] = part


def gather_sides(scratch, y_ref, blocks):
    size = blocks * RHS
    low = iota((blocks, LANES), 1) < LANES // 2
    for h in range(0, RHS, 2):
        one, two, three, four = (
            scratch[pl.ds(side * size + h + k, blocks, stride=RHS), :]
            for k in range(2)
            for side in range(2)
        )
        three, four = turn(three), turn(four)
        pair = (one, jnp.where(low, two, three), jnp.where(low, three, four))
        for j in range(3):
            at = h * TILE + j * LANES
            y_ref[:, at : at + LANES] = pair[j].astype(BF16)


def join(scratch, size):
    return jnp.concatenate(
        [scratch[side * size : (side + 1) * size, :].astype(BF16) for side in range(2)], axis=1
    )


def project(fields, basis_ref, coef_s):
    cols = GROUP * RANK
    lane = iota((RHS, LANES), 1) // RANK
    for g, field in enumerate(fields):
        cross = lax.dot_general(
            field, basis_ref[g * cols : (g + 1) * cols, :], NT, preferred_element_type=F32
        )
        for half in range(GROUP // SIDE):
            out = None
            for j in range(SIDE):
                at = (half * SIDE + j) * RHS
                part = cross[at : at + RHS, half * LANES : (half + 1) * LANES]
                out = part if out is None else jnp.where(lane == j, part, out)
            at = (g * (GROUP // SIDE) + half) * RHS
            for j in range(coef_s.shape[0]):
                coef_s[j, at : at + RHS, :] = out.astype(BF16)


def opening_kernel(
    v_hbm, b_hbm, lo_ref, hi_ref, basis_ref, coef_hbm, v_s, b_s, f_s, g_s, coef_s, sems
):
    gets = copies(((v_hbm, v_s), (b_hbm, b_s)), sems)
    put = copies(((coef_s, coef_hbm),), sems, 2)
    start(gets)
    blocks = v_s.shape[0]
    rows, ranks = blocks * RHS, blocks * RANK
    gets[0].wait()
    spread(v_s, f_s, blocks, RHS)
    field = join(f_s, rows)
    rim = RIM * RHS
    lo_ref[...] = field[:rim]
    hi_ref[...] = field[rim:]
    gets[1].wait()
    spread(b_s, g_s, blocks, RANK)
    basis_ref[...] = join(g_s, ranks)
    project((field[:rim], field[rim:]), basis_ref, coef_s)
    start(put)
    wait(put)


def place(at_s, kind_s, e_s, p_s, unroll):
    blocks, slots = at_s.shape

    def one_block(i, _):
        row = pl.multiple_of(i * RHS, RHS)
        for k in range(slots):
            source = pl.multiple_of(at_s[i, k], RHS)
            column = pl.multiple_of(kind_s[i, k], WIDE)
            p_s[pl.ds(row, RHS), pl.ds(column, WIDE)] = e_s[pl.ds(source, RHS), :]
        return 0

    lax.fori_loop(0, blocks, one_block, 0, unroll=unroll)


def multiply(p_s, table_s, out_ref, chunk):
    size, columns = out_ref.shape[0], table_s.shape[1]
    out_ref[:, LANES:] = jnp.zeros((size, LANES), F32)

    def some_columns(n, total):
        at = pl.multiple_of(n * chunk, chunk)
        return total + lax.dot_general(
            p_s[:, pl.ds(at, chunk)], table_s[:, pl.ds(at, chunk)], NT, preferred_element_type=F32
        )

    total = jnp.zeros((size, TILE), F32)
    out_ref[:, :TILE] = lax.fori_loop(0, columns // chunk, some_columns, total)


def first_near_kernel(
    slabs, slab_blocks,
    count_hbm, src_hbm, type_hbm, far_hbm, tiles_hbm, coup_hbm, lo_ref, hi_ref, chip_ref, further_ref,
    near_ref, mat_ref, table_hbm, far_idx_hbm, at_hbm, kind_hbm,
    count_s, src_s, type_s, far_s, tiles_s, coup_s, far_idx_s, at_v, kind_v, at_s, kind_s,
    h_s, e_s, p_s, table_s, sems,
):
    gets = copies(
        (
            (count_hbm, count_s),
            (src_hbm, src_s),
            (type_hbm, type_s),
            (far_hbm, far_s),
            (coup_hbm, coup_s),
            (tiles_hbm, tiles_s),
        ),
        sems,
    )
    puts = copies(
        (
            (at_v, at_s),
            (kind_v, kind_s),
            (at_v, at_hbm),
            (kind_v, kind_hbm),
            (far_idx_s, far_idx_hbm),
        ),
        sems,
        len(gets),
    )
    start(gets)
    types = tiles_s.shape[0]
    blocks, partners, _ = coup_s.shape
    deep = partners // SIDE
    size, rim = blocks * RHS, RIM * RHS
    me = lax.axis_index("slab")
    odd = me % 2 == 1

    p_s[:, : types * WIDE] = jnp.zeros((size, types * WIDE), BF16)
    e_s[:rim, :] = lo_ref[...]
    e_s[rim : 2 * rim, :] = hi_ref[...]
    for j, (ref, late) in enumerate(((chip_ref, odd), (further_ref, ~odd))):
        spread(ref, h_s, RIM, RHS, late)
        e_s[(2 + j) * rim : (3 + j) * rim, :] = join(h_s, rim)

    wait(gets[:4])
    source = src_s[...]
    step = (source // slab_blocks - me + slabs) % slabs
    after = jnp.where(odd, 3 * RIM, 2 * RIM)
    before = jnp.where(odd, RIM, 2 * RIM)
    offset = jnp.where(step == 0, 0, jnp.where(step == 1, after, before))
    at_v[...] = (source % blocks + offset) * RHS
    row = iota(source.shape, 0)
    count = jnp.zeros(source.shape, jnp.int32)
    for i in range(blocks):
        count = jnp.where(row == i, count_s[i], count)
    kind_v[...] = jnp.where(iota(source.shape, 1) < count, type_s[...], types) * WIDE

    source = far_s[...] % slab_blocks
    group = iota(source.shape, 1) // deep
    turned = (group - source) & (SIDE - 1)
    far_idx_s[...] = (turned * (slab_blocks // SIDE) + source // SIDE) * RHS
    start(puts)

    lane = iota((deep, LANES), 1) // RANK
    order = swap(RANK * deep, RANK)
    gets[4].wait()

    def two_blocks(n, _):
        stacks = []
        for b in range(2):
            i = 2 * n + b
            stack = []
            for big in range(RANK // SIDE):
                x = coup_s[i, :, big * LANES : (big + 1) * LANES].astype(F32)
                parts = [x[j * deep : (j + 1) * deep] for j in range(SIDE)]
                turned = [
                    [p if r == 0 else pltpu.roll(p, r * RANK, 1) for r in range(SIDE)]
                    for p in parts
                ]
                for small in range(SIDE):
                    out = turned[0][-small % SIDE]
                    for j in range(1, SIDE):
                        out = jnp.where(lane == j, turned[j][(j - small) % SIDE], out)
                    stack.append(out)
            stacks.append(jnp.concatenate(stack, axis=0).astype(BF16))
        both = jnp.concatenate(stacks, axis=1)
        both = lax.dot_general(order, both, NN, preferred_element_type=F32).astype(BF16)
        for b in range(2):
            at = pl.multiple_of((2 * n + b) * RANK, RANK)
            for k in range(deep):
                part = both[k * RANK : (k + 1) * RANK, b * LANES : (b + 1) * LANES]
                mat_ref[pl.ds(at, RANK), k * LANES : (k + 1) * LANES] = part
        return 0

    lax.fori_loop(0, blocks // 2, two_blocks, 0, unroll=True)

    wait(puts[:2])
    place(at_s, kind_s, e_s, p_s, True)

    many = 16
    order = swap(many * many, many)
    gets[5].wait()

    low = iota((many, LANES), 1) < LANES // 2
    steps = STEPS
    each = TILE // steps
    put_table = [
        copies(((table_s.at[rows], table_hbm.at[rows]),), sems, 11 + n)
        for n, rows in enumerate(pl.ds(n * each, each) for n in range(steps))
    ]

    def some_rows(step, _):
        for n in range(each // many):
            at = pl.multiple_of(step * (each * TILE), LANES) + n * many * TILE
            for a in range(types // many):
                stack = []
                for d in range(0, many, 2):
                    one, two, three = (
                        tiles_s[a * many : (a + 1) * many, pl.ds(at + d * TILE + j * LANES, LANES)]
                        for j in range(3)
                    )
                    two_turned, three_turned = turn(two), turn(three)
                    stack.append(jnp.concatenate((one, two), axis=1))
                    mixed = jnp.where(low, two_turned, three_turned)
                    stack.append(jnp.concatenate((mixed, three_turned), axis=1))
                out = jnp.concatenate(stack, axis=0)
                out = lax.dot_general(order, out, NN, preferred_element_type=F32).astype(BF16)
                for t in range(many):
                    to = (a * many + t) * WIDE
                    row = pl.multiple_of(step * each + n * many, many)
                    table_s[pl.ds(row, many), to : to + WIDE] = out[t * many : (t + 1) * many]
        rows = pl.ds(pl.multiple_of(step * each, many), each)
        start(copies(((table_s.at[rows], table_hbm.at[rows]),), sems, 11 + step))
        return 0

    lax.fori_loop(0, steps, some_rows, 0)
    multiply(p_s, table_s, near_ref, table_s.shape[1] // 2)
    wait(puts[2:])
    for put in put_table:
        wait(put)


def second_near_kernel(
    at_hbm, kind_hbm, lo_ref, hi_ref, chip_ref, further_ref, table_hbm,
    near_ref, y_hbm,
    at_s, kind_s, e_s, p_s, table_s, f_s, y_s, sems,
):
    gets = copies(((at_hbm, at_s), (kind_hbm, kind_s), (table_hbm, table_s)), sems)
    put = copies(((y_s, y_hbm),), sems, len(gets))
    start(gets)
    blocks = at_s.shape[0]
    size, rim = blocks * RHS, RIM * RHS
    for j, ref in enumerate((lo_ref, hi_ref, chip_ref, further_ref)):
        e_s[j * rim : (j + 1) * rim, :] = ref[...]
    for j in range(2):
        f_s[j * size : (j + 1) * size, :] = e_s[:size, j * LANES : (j + 1) * LANES].astype(F32)
    gather_sides(f_s, y_s, blocks)
    start(put)
    columns = table_s.shape[1]
    p_s[:, :columns] = jnp.zeros((size, columns), BF16)
    wait(gets[:2])
    place(at_s, kind_s, e_s, p_s, True)
    gets[2].wait()
    multiply(p_s, table_s, near_ref, table_s.shape[1])
    wait(put)


def far_kernel(last, idx_hbm, got_any, mat_ref, basis_ref, near_ref, *rest):
    if last:
        y_ref, idx_s, got_ref, turn_s, pick_s, sem, sum_s = rest
    else:
        lo_ref, hi_ref, chip_ref, further_ref, coef_hbm, idx_s, got_ref, turn_s, pick_s, sem, coef_s = rest
        put = copies(((coef_s, coef_hbm),), sem, 2)
    gets = copies(((got_any, got_ref), (idx_hbm, idx_s)), sem)
    start(gets)
    gets[0].wait()
    blocks, partners = idx_s.shape
    deep = partners // SIDE
    peers, packed_rows, _ = got_ref.shape
    quarter = peers * packed_rows
    for j in range(peers):
        got = got_ref[j]
        for r in range(SIDE):
            at = r * quarter + j * packed_rows
            turn_s[at : at + packed_rows, :] = got if r == 0 else pltpu.roll(got, r * RANK, 1)
    lane = iota((RHS, LANES), 1) // RANK
    gets[1].wait()

    def one_block(i, _):
        row = pl.multiple_of(i * RHS, RHS)
        for k in range(deep):
            out = None
            for j in range(SIDE):
                at = pl.multiple_of(idx_s[i, j * deep + k], RHS)
                part = turn_s[pl.ds(at, RHS), :]
                out = part if out is None else jnp.where(lane == j, part, out)
            pick_s[pl.ds(row, RHS), k * LANES : (k + 1) * LANES] = out
        return 0

    lax.fori_loop(0, blocks, one_block, 0, unroll=True)
    size = blocks * RHS
    rows, cols = GROUP * RHS, GROUP * RANK
    own = iota((rows, cols), 0) // RHS == iota((rows, cols), 1) // RANK
    fields = []
    for g in range(blocks // GROUP):
        cross = lax.dot_general(
            pick_s[g * rows : (g + 1) * rows, :],
            mat_ref[g * cols : (g + 1) * cols, :],
            NT,
            preferred_element_type=F32,
        )
        mix = jnp.where(own, cross, 0.0).astype(BF16)
        far = lax.dot_general(
            mix, basis_ref[g * cols : (g + 1) * cols, :], NN, preferred_element_type=F32
        )
        total = near_ref[g * rows : (g + 1) * rows, :] + far
        if last:
            for j in range(2):
                at = j * size + g * rows
                sum_s[at : at + rows, :] = total[:, j * LANES : (j + 1) * LANES]
        else:
            fields.append(total.astype(BF16))
    if last:
        gather_sides(sum_s, y_ref, blocks)
    else:
        project(fields, basis_ref, coef_s)
        start(put)
        lo_ref[...], hi_ref[...] = lo, hi = fields
        odd = lax.axis_index("slab") % 2 == 1
        chip_ref[...] = jnp.where(odd, lo, hi)
        further_ref[...] = jnp.where(odd, hi, lo)
        wait(put)


def opening(peers, vectors, bases):
    blocks = vectors.shape[0]
    rows, ranks, rim = blocks * RHS, blocks * RANK, RIM * RHS
    field = (shape((rim, WIDE), BF16), VMEM)
    coef = (peers, rows // SIDE, LANES)
    return call(
        opening_kernel, "opening", (vectors, bases), [HBM] * 2,
        [field, field, (shape((ranks, WIDE), BF16), VMEM), (shape(coef, BF16), HBM)],
        [
            pltpu.VMEM(vectors.shape, BF16),
            pltpu.VMEM(bases.shape, BF16),
            pltpu.VMEM((2 * rows, LANES), F32),
            pltpu.VMEM((2 * ranks, LANES), F32),
            pltpu.VMEM(coef, BF16),
            pltpu.SemaphoreType.DMA((3,)),
        ],
        8,
    )


def first_near(
    slabs, peers, near_count, near_src, near_type, far_src, tiles, coupling, lo, hi, chip, further
):
    blocks, partners, _ = coupling.shape
    rows, rim = blocks * RHS, RIM * RHS
    types = tiles.shape[0]
    table = (TILE, types * WIDE)
    slots = (near_src.shape, jnp.int32)
    picks = (far_src.shape, jnp.int32)
    return call(
        functools.partial(first_near_kernel, slabs, blocks * peers), "first_near",
        (near_count, near_src, near_type, far_src, tiles, coupling, lo, hi, chip, further),
        [HBM] * 6 + [VMEM] * 4,
        [
            (shape((rows, WIDE), F32), VMEM),
            (shape((blocks * RANK, partners * RANK), BF16), VMEM),
            (shape(table, BF16), HBM),
            (shape(*picks), HBM),
            (shape(*slots), HBM),
            (shape(*slots), HBM),
        ],
        [
            pltpu.SMEM(near_count.shape, jnp.int32),
            pltpu.VMEM(*slots),
            pltpu.VMEM(*slots),
            pltpu.VMEM(*picks),
            pltpu.VMEM(tiles.shape, BF16),
            pltpu.VMEM(coupling.shape, BF16),
            pltpu.VMEM(*picks),
            pltpu.VMEM(*slots),
            pltpu.VMEM(*slots),
            pltpu.SMEM(*slots),
            pltpu.SMEM(*slots),
            pltpu.VMEM((2 * rim, LANES), F32),
            pltpu.VMEM((4 * rim, WIDE), BF16),
            pltpu.VMEM((rows, (types + 1) * WIDE), BF16),
            pltpu.VMEM(table, BF16),
            pltpu.SemaphoreType.DMA((11 + STEPS,)),
        ],
        20, LONG,
    )


def second_near(at, kind, lo, hi, chip, further, table):
    rim = lo.shape[0]
    rows = 2 * rim
    y = (rows // RHS, RHS * TILE)
    return call(
        second_near_kernel, "second_near", (at, kind, lo, hi, chip, further, table),
        [HBM] * 2 + [VMEM] * 4 + [HBM],
        [(shape((rows, WIDE), F32), VMEM), (shape(y, BF16), HBM)],
        [
            pltpu.SMEM(at.shape, jnp.int32),
            pltpu.SMEM(at.shape, jnp.int32),
            pltpu.VMEM((2 * rows, WIDE), BF16),
            pltpu.VMEM((rows, table.shape[1] + WIDE), BF16),
            pltpu.VMEM(table.shape, BF16),
            pltpu.VMEM((2 * rows, LANES), F32),
            pltpu.VMEM(y, BF16),
            pltpu.SemaphoreType.DMA((4,)),
        ],
        16, 12_000_000,
    )


def far(last, idx, got, mat, basis, near_term):
    rows = near_term.shape[0]
    peers, packed, _ = got.shape
    scratch = [
        pltpu.SMEM(idx.shape, jnp.int32),
        pltpu.VMEM(got.shape, BF16),
        pltpu.VMEM((SIDE * peers * packed, LANES), BF16),
        pltpu.VMEM((rows, mat.shape[1]), BF16),
        pltpu.SemaphoreType.DMA((3,)),
    ]
    if last:
        outs = [(shape((rows // RHS, RHS * TILE), BF16), VMEM)]
        scratch.append(pltpu.VMEM((2 * rows, LANES), F32))
    else:
        outs = [(shape((rows // 2, WIDE), BF16), VMEM)] * 4 + [(shape(got.shape, BF16), HBM)]
        scratch.append(pltpu.VMEM(got.shape, BF16))
    return call(
        functools.partial(far_kernel, last), "far_last" if last else "far",
        (idx, got, mat, basis, near_term), [HBM, ANY] + [VMEM] * 3, outs, scratch, 8,
    )


def per_device(vectors, tiles, near_src, near_type, near_count, bases, far_src, coupling):
    slabs, peers = lax.axis_size("slab"), lax.axis_size("grp")
    chips = [(i, i ^ 1) for i in range(slabs)]
    between = [(i, (i + 1 if i % 2 else i - 1) % slabs) for i in range(slabs)]

    def halo(chip, further):
        return lax.ppermute(chip, "slab", chips), lax.ppermute(further, "slab", between)

    def exchange(coef):
        return lax.all_to_all(coef, "grp", 0, 0, tiled=True)

    chip, further = halo(vectors, vectors)
    lo, hi, basis, coef = opening(peers, vectors, bases)
    got = exchange(coef)
    near_term, mat, table, idx, at, kind = first_near(
        slabs, peers, near_count, near_src, near_type, far_src, tiles, coupling, lo, hi, chip, further
    )
    lo, hi, chip, further, coef = far(False, idx, got, mat, basis, near_term)
    got = exchange(coef)
    chip, further = halo(chip, further)
    near_term, first = second_near(at, kind, lo, hi, chip, further, table)
    (second,) = far(True, idx, got, mat, basis, near_term)
    return (first, second)


def solution(mesh):
    in_specs = (
        P(("slab", "grp"), None),
        P(),
        P(("slab", "grp"), None),
        P(("slab", "grp"), None),
        P(("slab", "grp")),
        P(("slab", "grp"), None),
        P(("slab", "grp"), None),
        P(("slab", "grp"), None, None),
    )
    out_specs = (P(("slab", "grp"), None), P(("slab", "grp"), None))
    return jax.shard_map(
        per_device, mesh=mesh, in_specs=in_specs, out_specs=out_specs, check_vma=False
    )
```

```python
import functools

import jax
import jax.numpy as jnp
from jax import lax
from jax.experimental import pallas as pl
from jax.experimental.pallas import tpu as pltpu
from jax.sharding import PartitionSpec as P

TILE = 192
RHS = 16
RANK = 32
RIM = 8
LANES = 128
WIDE = 256
GROUP = 8
LONG = 100_000_000
STEPS = 2
SIDE = LANES // RANK

VMEM = pl.BlockSpec(memory_space=pltpu.VMEM)
SMEM = pl.BlockSpec(memory_space=pltpu.SMEM)
HBM = pl.BlockSpec(memory_space=pltpu.HBM)
ANY = pl.BlockSpec(memory_space=pl.ANY)
KEPT = pl.BlockSpec(memory_space=pltpu.VMEM)
BOUND = (HBM, SMEM, KEPT)
F32 = jnp.float32
BF16 = jnp.bfloat16
NT = (((1,), (1,)), ((), ()))
NN = (((1,), (0,)), ((), ()))
shape = jax.ShapeDtypeStruct


def call(kernel, name, args, ins, outs, scratch, mib, moved=0):
    args = [
        pltpu.with_memory_space_constraint(a, s.memory_space) if any(s is b for b in BOUND) else a
        for a, s in zip(args, ins)
    ]
    return pl.pallas_call(
        kernel,
        out_shape=tuple(
            s.memory_space(o.shape, o.dtype) if any(s is b for b in BOUND) else o for o, s in outs
        ),
        in_specs=ins,
        out_specs=tuple(s for _, s in outs),
        scratch_shapes=scratch,
        compiler_params=pltpu.CompilerParams(vmem_limit_bytes=mib * 1024 * 1024),
        cost_estimate=pl.CostEstimate(flops=100 * moved, bytes_accessed=moved, transcendentals=0),
        name=name,
    )(*args)


def copies(pairs, sems, first=0):
    return [
        pltpu.make_async_copy(source, to, sems.at[first + j]) for j, (source, to) in enumerate(pairs)
    ]


def start(group):
    for copy in group:
        copy.start()


def wait(group):
    for copy in group:
        copy.wait()


def iota(shape, axis):
    return lax.broadcasted_iota(jnp.int32, shape, axis)


def swap(rows, outer):
    at = iota((rows, rows), 0)
    source = (at % outer) * (rows // outer) + at // outer
    return (iota((rows, rows), 1) == source).astype(BF16)


def turn(x):
    return pltpu.roll(x, LANES // 2, 1)


def halves(pair):
    low = iota((pair.shape[0], LANES), 1) < LANES // 2
    one, two, three = (pair[:, j * LANES : (j + 1) * LANES] for j in range(3))
    two_turned, three_turned = turn(two), turn(three)
    zero = jnp.zeros_like(two)
    return (
        (one, jnp.where(low, two, zero)),
        (jnp.where(low, two_turned, three_turned), jnp.where(low, three_turned, zero)),
    )


def spread(source_ref, scratch, rows, count, late=None):
    size = rows * count
    for j in range(0, count, 2):
        pair = source_ref[:, j * TILE : (j + 2) * TILE].astype(F32)
        if late is not None:
            pair = jnp.where(late, pair[rows:], pair[:rows])
        for k, parts in enumerate(halves(pair)):
            for side, part in enumerate(parts):
                scratch[pl.ds(side * size + j + k, rows, stride=count), :] = part


def gather_sides(scratch, y_ref, blocks):
    size = blocks * RHS
    low = iota((blocks, LANES), 1) < LANES // 2
    for h in range(0, RHS, 2):
        one, two, three, four = (
            scratch[pl.ds(side * size + h + k, blocks, stride=RHS), :]
            for k in range(2)
            for side in range(2)
        )
        three, four = turn(three), turn(four)
        pair = (one, jnp.where(low, two, three), jnp.where(low, three, four))
        for j in range(3):
            at = h * TILE + j * LANES
            y_ref[:, at : at + LANES] = pair[j].astype(BF16)


def join(scratch, size):
    return jnp.concatenate(
        [scratch[side * size : (side + 1) * size, :].astype(BF16) for side in range(2)], axis=1
    )


def project(fields, basis_ref, coef_s):
    cols = GROUP * RANK
    lane = iota((RHS, LANES), 1) // RANK
    crosses = [
        lax.dot_general(
            field, basis_ref[g * cols : (g + 1) * cols, :], NT, preferred_element_type=F32
        )
        for g, field in enumerate(fields)
    ]
    for g, cross in enumerate(crosses):
        for half in range(GROUP // SIDE):
            out = None
            for j in range(SIDE):
                at = (half * SIDE + j) * RHS
                part = cross[at : at + RHS, half * LANES : (half + 1) * LANES]
                out = part if out is None else jnp.where(lane == j, part, out)
            at = (g * (GROUP // SIDE) + half) * RHS
            for j in range(coef_s.shape[0]):
                coef_s[j, at : at + RHS, :] = out.astype(BF16)


def opening_kernel(
    v_hbm, b_hbm, lo_ref, hi_ref, basis_ref, coef_hbm, v_s, b_s, f_s, g_s, coef_s, sems
):
    gets = copies(((v_hbm, v_s), (b_hbm, b_s)), sems)
    put = copies(((coef_s, coef_hbm),), sems, 2)
    start(gets)
    blocks = v_s.shape[0]
    rows, ranks = blocks * RHS, blocks * RANK
    gets[0].wait()
    spread(v_s, f_s, blocks, RHS)
    field = join(f_s, rows)
    rim = RIM * RHS
    lo_ref[...] = field[:rim]
    hi_ref[...] = field[rim:]
    gets[1].wait()
    spread(b_s, g_s, blocks, RANK)
    basis_ref[...] = join(g_s, ranks)
    project((field[:rim], field[rim:]), basis_ref, coef_s)
    start(put)
    wait(put)


def place(at_s, kind_s, e_s, p_s, unroll):
    blocks, slots = at_s.shape

    def one_block(i, _):
        row = pl.multiple_of(i * RHS, RHS)
        for k in range(slots):
            source = pl.multiple_of(at_s[i, k], RHS)
            column = pl.multiple_of(kind_s[i, k], WIDE)
            p_s[pl.ds(row, RHS), pl.ds(column, WIDE)] = e_s[pl.ds(source, RHS), :]
        return 0

    lax.fori_loop(0, blocks, one_block, 0, unroll=unroll)


def multiply(p_s, table_s, out_ref, chunk):
    size, columns = out_ref.shape[0], table_s.shape[1]
    out_ref[:, LANES:] = jnp.zeros((size, LANES), F32)

    def some_columns(n, total):
        at = pl.multiple_of(n * chunk, chunk)
        return total + lax.dot_general(
            p_s[:, pl.ds(at, chunk)], table_s[:, pl.ds(at, chunk)], NT, preferred_element_type=F32
        )

    total = jnp.zeros((size, TILE), F32)
    out_ref[:, :TILE] = lax.fori_loop(0, columns // chunk, some_columns, total)


def first_near_kernel(
    slabs, slab_blocks,
    count_hbm, src_hbm, type_hbm, far_hbm, tiles_hbm, coup_hbm, lo_ref, hi_ref, chip_ref, further_ref,
    near_ref, mat_ref, table_hbm, far_idx_ref, at_s, kind_s,
    count_s, src_s, type_s, far_s, tiles_s, coup_s, far_idx_s, at_v, kind_v,
    h_s, e_s, p_s, table_s, sems,
):
    gets = copies(
        (
            (count_hbm, count_s),
            (src_hbm, src_s),
            (type_hbm, type_s),
            (far_hbm, far_s),
            (coup_hbm, coup_s),
            (tiles_hbm, tiles_s),
        ),
        sems,
    )
    puts = copies(
        (
            (at_v, at_s),
            (kind_v, kind_s),
            (far_idx_s, far_idx_ref),
        ),
        sems,
        len(gets),
    )
    start(gets)
    types = tiles_s.shape[0]
    blocks, partners, _ = coup_s.shape
    deep = partners // SIDE
    size, rim = blocks * RHS, RIM * RHS
    me = lax.axis_index("slab")
    odd = me % 2 == 1

    p_s[:, : types * WIDE] = jnp.zeros((size, types * WIDE), BF16)
    e_s[:rim, :] = lo_ref[...]
    e_s[rim : 2 * rim, :] = hi_ref[...]
    for j, (ref, late) in enumerate(((chip_ref, odd), (further_ref, ~odd))):
        spread(ref, h_s, RIM, RHS, late)
        e_s[(2 + j) * rim : (3 + j) * rim, :] = join(h_s, rim)

    wait(gets[:4])
    source = src_s[...]
    step = (source // slab_blocks - me + slabs) % slabs
    after = jnp.where(odd, 3 * RIM, 2 * RIM)
    before = jnp.where(odd, RIM, 2 * RIM)
    offset = jnp.where(step == 0, 0, jnp.where(step == 1, after, before))
    at_v[...] = (source % blocks + offset) * RHS
    row = iota(source.shape, 0)
    count = jnp.zeros(source.shape, jnp.int32)
    for i in range(blocks):
        count = jnp.where(row == i, count_s[i], count)
    kind_v[...] = jnp.where(iota(source.shape, 1) < count, type_s[...], types) * WIDE

    source = far_s[...] % slab_blocks
    group = iota(source.shape, 1) // deep
    turned = (group - source) & (SIDE - 1)
    far_idx_s[...] = (turned * (slab_blocks // SIDE) + source // SIDE) * RHS
    start(puts)

    lane = iota((deep, LANES), 1) // RANK
    order = swap(RANK * deep, RANK)
    gets[4].wait()

    def two_blocks(n, _):
        stacks = []
        for b in range(2):
            i = 2 * n + b
            stack = []
            for big in range(RANK // SIDE):
                x = coup_s[i, :, big * LANES : (big + 1) * LANES].astype(F32)
                parts = [x[j * deep : (j + 1) * deep] for j in range(SIDE)]
                turned = [
                    [p if r == 0 else pltpu.roll(p, r * RANK, 1) for r in range(SIDE)]
                    for p in parts
                ]
                for small in range(SIDE):
                    out = turned[0][-small % SIDE]
                    for j in range(1, SIDE):
                        out = jnp.where(lane == j, turned[j][(j - small) % SIDE], out)
                    stack.append(out)
            stacks.append(jnp.concatenate(stack, axis=0).astype(BF16))
        both = jnp.concatenate(stacks, axis=1)
        both = lax.dot_general(order, both, NN, preferred_element_type=F32).astype(BF16)
        for b in range(2):
            at = pl.multiple_of((2 * n + b) * RANK, RANK)
            for k in range(deep):
                part = both[k * RANK : (k + 1) * RANK, b * LANES : (b + 1) * LANES]
                mat_ref[pl.ds(at, RANK), k * LANES : (k + 1) * LANES] = part
        return 0

    lax.fori_loop(0, blocks // 2, two_blocks, 0, unroll=True)

    wait(puts[:2])
    place(at_s, kind_s, e_s, p_s, True)

    many = 16
    order = swap(many * many, many)
    gets[5].wait()

    low = iota((many, LANES), 1) < LANES // 2
    steps = STEPS
    each = TILE // steps
    put_table = [
        copies(((table_s.at[rows], table_hbm.at[rows]),), sems, 9 + n)
        for n, rows in enumerate(pl.ds(n * each, each) for n in range(steps))
    ]

    def some_rows(step, _):
        for n in range(each // many):
            at = pl.multiple_of(step * (each * TILE), LANES) + n * many * TILE
            for a in range(types // many):
                stack = []
                for d in range(0, many, 2):
                    one, two, three = (
                        tiles_s[a * many : (a + 1) * many, pl.ds(at + d * TILE + j * LANES, LANES)]
                        for j in range(3)
                    )
                    two_turned, three_turned = turn(two), turn(three)
                    stack.append(jnp.concatenate((one, two), axis=1))
                    mixed = jnp.where(low, two_turned, three_turned)
                    stack.append(jnp.concatenate((mixed, three_turned), axis=1))
                out = jnp.concatenate(stack, axis=0)
                out = lax.dot_general(order, out, NN, preferred_element_type=F32).astype(BF16)
                for t in range(many):
                    to = (a * many + t) * WIDE
                    row = pl.multiple_of(step * each + n * many, many)
                    table_s[pl.ds(row, many), to : to + WIDE] = out[t * many : (t + 1) * many]
        rows = pl.ds(pl.multiple_of(step * each, many), each)
        start(copies(((table_s.at[rows], table_hbm.at[rows]),), sems, 9 + step))
        return 0

    lax.fori_loop(0, steps, some_rows, 0)
    multiply(p_s, table_s, near_ref, table_s.shape[1] // 2)
    wait(puts[2:])
    for put in put_table:
        wait(put)


def give_kernel(lo_ref, hi_ref, table_hbm, y_hbm, table_ref, f_s, y_s, sems):
    gets = copies(((table_hbm, table_ref),), sems)
    put = copies(((y_s, y_hbm),), sems, 1)
    start(gets)
    rim = lo_ref.shape[0]
    for k, ref in enumerate((lo_ref, hi_ref)):
        for j in range(2):
            at = (2 * j + k) * rim
            f_s[at : at + rim, :] = ref[:, j * LANES : (j + 1) * LANES].astype(F32)
    gather_sides(f_s, y_s, y_s.shape[0])
    start(put)
    wait(gets + put)


def second_near_kernel(
    at_s, kind_s, lo_ref, hi_ref, chip_ref, further_ref, table_ref, near_ref, e_s, p_s
):
    rim, columns = RIM * RHS, table_ref.shape[1]
    for j, ref in enumerate((lo_ref, hi_ref, chip_ref, further_ref)):
        e_s[j * rim : (j + 1) * rim, :] = ref[...]
    p_s[:, :columns] = jnp.zeros((p_s.shape[0], columns), BF16)
    place(at_s, kind_s, e_s, p_s, True)
    multiply(p_s, table_ref, near_ref, columns)


def far_kernel(last, idx_s, got_any, mat_ref, basis_ref, near_ref, *rest):
    if last:
        y_ref, got_ref, turn_s, pick_s, sem, sum_s = rest
    else:
        lo_ref, hi_ref, chip_ref, further_ref, coef_hbm, got_ref, turn_s, pick_s, sem, coef_s = rest
        put = copies(((coef_s, coef_hbm),), sem, 1)
    gets = copies(((got_any, got_ref),), sem)
    start(gets)
    wait(gets)
    blocks, partners = idx_s.shape
    deep = partners // SIDE
    peers, packed_rows, _ = got_ref.shape
    quarter = peers * packed_rows
    for j in range(peers):
        got = got_ref[j]
        for r in range(SIDE):
            at = r * quarter + j * packed_rows
            turn_s[at : at + packed_rows, :] = got if r == 0 else pltpu.roll(got, r * RANK, 1)
    lane = iota((RHS, LANES), 1) // RANK

    def one_block(i, _):
        row = pl.multiple_of(i * RHS, RHS)
        for k in range(deep):
            out = None
            for j in range(SIDE):
                at = pl.multiple_of(idx_s[i, j * deep + k], RHS)
                part = turn_s[pl.ds(at, RHS), :]
                out = part if out is None else jnp.where(lane == j, part, out)
            pick_s[pl.ds(row, RHS), k * LANES : (k + 1) * LANES] = out
        return 0

    lax.fori_loop(0, blocks, one_block, 0, unroll=True)
    size = blocks * RHS
    rows, cols = GROUP * RHS, GROUP * RANK
    own = iota((rows, cols), 0) // RHS == iota((rows, cols), 1) // RANK
    groups = range(blocks // GROUP)
    crosses = [
        lax.dot_general(
            pick_s[g * rows : (g + 1) * rows, :],
            mat_ref[g * cols : (g + 1) * cols, :],
            NT,
            preferred_element_type=F32,
        )
        for g in groups
    ]
    mixes = [jnp.where(own, cross, 0.0).astype(BF16) for cross in crosses]
    totals = [
        near_ref[g * rows : (g + 1) * rows, :]
        + lax.dot_general(
            mixes[g], basis_ref[g * cols : (g + 1) * cols, :], NN, preferred_element_type=F32
        )
        for g in groups
    ]
    if last:
        for g in groups:
            for j in range(2):
                at = j * size + g * rows
                sum_s[at : at + rows, :] = totals[g][:, j * LANES : (j + 1) * LANES]
    fields = [total.astype(BF16) for total in totals]
    if last:
        gather_sides(sum_s, y_ref, blocks)
    else:
        project(fields, basis_ref, coef_s)
        start(put)
        lo_ref[...], hi_ref[...] = lo, hi = fields
        odd = lax.axis_index("slab") % 2 == 1
        chip_ref[...] = jnp.where(odd, lo, hi)
        further_ref[...] = jnp.where(odd, hi, lo)
        wait(put)


def opening(peers, vectors, bases):
    blocks = vectors.shape[0]
    rows, ranks, rim = blocks * RHS, blocks * RANK, RIM * RHS
    field = (shape((rim, WIDE), BF16), VMEM)
    coef = (peers, rows // SIDE, LANES)
    return call(
        opening_kernel, "opening", (vectors, bases), [HBM] * 2,
        [field, field, (shape((ranks, WIDE), BF16), VMEM), (shape(coef, BF16), HBM)],
        [
            pltpu.VMEM(vectors.shape, BF16),
            pltpu.VMEM(bases.shape, BF16),
            pltpu.VMEM((2 * rows, LANES), F32),
            pltpu.VMEM((2 * ranks, LANES), F32),
            pltpu.VMEM(coef, BF16),
            pltpu.SemaphoreType.DMA((3,)),
        ],
        8,
    )


def first_near(
    slabs, peers, near_count, near_src, near_type, far_src, tiles, coupling, lo, hi, chip, further
):
    blocks, partners, _ = coupling.shape
    rows, rim = blocks * RHS, RIM * RHS
    types = tiles.shape[0]
    table = (TILE, types * WIDE)
    slots = (near_src.shape, jnp.int32)
    picks = (far_src.shape, jnp.int32)
    return call(
        functools.partial(first_near_kernel, slabs, blocks * peers), "first_near",
        (near_count, near_src, near_type, far_src, tiles, coupling, lo, hi, chip, further),
        [HBM] * 6 + [VMEM] * 4,
        [
            (shape((rows, WIDE), F32), VMEM),
            (shape((blocks * RANK, partners * RANK), BF16), VMEM),
            (shape(table, BF16), HBM),
            (shape(*picks), SMEM),
            (shape(*slots), SMEM),
            (shape(*slots), SMEM),
        ],
        [
            pltpu.SMEM(near_count.shape, jnp.int32),
            pltpu.VMEM(*slots),
            pltpu.VMEM(*slots),
            pltpu.VMEM(*picks),
            pltpu.VMEM(tiles.shape, BF16),
            pltpu.VMEM(coupling.shape, BF16),
            pltpu.VMEM(*picks),
            pltpu.VMEM(*slots),
            pltpu.VMEM(*slots),
            pltpu.VMEM((2 * rim, LANES), F32),
            pltpu.VMEM((4 * rim, WIDE), BF16),
            pltpu.VMEM((rows, (types + 1) * WIDE), BF16),
            pltpu.VMEM(table, BF16),
            pltpu.SemaphoreType.DMA((9 + STEPS,)),
        ],
        20, LONG,
    )


def give(lo, hi, table):
    rows = 2 * lo.shape[0]
    y = (rows // RHS, RHS * TILE)
    return call(
        give_kernel, "give", (lo, hi, table), [VMEM] * 2 + [HBM],
        [(shape(y, BF16), HBM), (shape(table.shape, BF16), KEPT)],
        [
            pltpu.VMEM((2 * rows, LANES), F32),
            pltpu.VMEM(y, BF16),
            pltpu.SemaphoreType.DMA((2,)),
        ],
        4, 12_000_000,
    )


def second_near(at, kind, lo, hi, chip, further, table):
    rows = 2 * lo.shape[0]
    return call(
        second_near_kernel, "second_near", (at, kind, lo, hi, chip, further, table),
        [SMEM] * 2 + [VMEM] * 4 + [KEPT],
        [(shape((rows, WIDE), F32), VMEM)],
        [
            pltpu.VMEM((2 * rows, WIDE), BF16),
            pltpu.VMEM((rows, table.shape[1] + WIDE), BF16),
        ],
        8, 12_000_000,
    )[0]


def far(last, idx, got, mat, basis, near_term):
    rows = near_term.shape[0]
    peers, packed, _ = got.shape
    scratch = [
        pltpu.VMEM(got.shape, BF16),
        pltpu.VMEM((SIDE * peers * packed, LANES), BF16),
        pltpu.VMEM((rows, mat.shape[1]), BF16),
        pltpu.SemaphoreType.DMA((2,)),
    ]
    if last:
        outs = [(shape((rows // RHS, RHS * TILE), BF16), VMEM)]
        scratch.append(pltpu.VMEM((2 * rows, LANES), F32))
    else:
        outs = [(shape((rows // 2, WIDE), BF16), VMEM)] * 4 + [(shape(got.shape, BF16), HBM)]
        scratch.append(pltpu.VMEM(got.shape, BF16))
    return call(
        functools.partial(far_kernel, last), "far_last" if last else "far",
        (idx, got, mat, basis, near_term), [SMEM, ANY] + [VMEM] * 3, outs, scratch, 8,
    )


def per_device(vectors, tiles, near_src, near_type, near_count, bases, far_src, coupling):
    slabs, peers = lax.axis_size("slab"), lax.axis_size("grp")
    chips = [(i, i ^ 1) for i in range(slabs)]
    between = [(i, (i + 1 if i % 2 else i - 1) % slabs) for i in range(slabs)]

    def halo(chip, further):
        return lax.ppermute(chip, "slab", chips), lax.ppermute(further, "slab", between)

    def exchange(coef):
        return lax.all_to_all(coef, "grp", 0, 0, tiled=True)

    chip, further = halo(vectors, vectors)
    lo, hi, basis, coef = opening(peers, vectors, bases)
    got = exchange(coef)
    near_term, mat, table, idx, at, kind = first_near(
        slabs, peers, near_count, near_src, near_type, far_src, tiles, coupling, lo, hi, chip, further
    )
    lo, hi, chip, further, coef = far(False, idx, got, mat, basis, near_term)
    got = exchange(coef)
    chip, further = halo(chip, further)
    first, table = give(lo, hi, table)
    near_term = second_near(at, kind, lo, hi, chip, further, table)
    (second,) = far(True, idx, got, mat, basis, near_term)
    return (first, second)


def solution(mesh):
    in_specs = (
        P(("slab", "grp"), None),
        P(),
        P(("slab", "grp"), None),
        P(("slab", "grp"), None),
        P(("slab", "grp")),
        P(("slab", "grp"), None),
        P(("slab", "grp"), None),
        P(("slab", "grp"), None, None),
    )
    out_specs = (P(("slab", "grp"), None), P(("slab", "grp"), None))
    return jax.shard_map(
        per_device, mesh=mesh, in_specs=in_specs, out_specs=out_specs, check_vma=False
    )
```

```python
import functools

import jax
import jax.numpy as jnp
from jax import lax
from jax.experimental import pallas as pl
from jax.experimental.pallas import tpu as pltpu
from jax.sharding import PartitionSpec as P

TILE = 192
RHS = 16
RANK = 32
RIM = 8
LANES = 128
WIDE = 256
GROUP = 8
LONG = 100_000_000
STEPS = 2
SIDE = LANES // RANK

VMEM = pl.BlockSpec(memory_space=pltpu.VMEM)
SMEM = pl.BlockSpec(memory_space=pltpu.SMEM)
HBM = pl.BlockSpec(memory_space=pltpu.HBM)
KEPT = pl.BlockSpec(memory_space=pltpu.VMEM)
BOUND = (HBM, SMEM, KEPT)
F32 = jnp.float32
BF16 = jnp.bfloat16
NT = (((1,), (1,)), ((), ()))
NN = (((1,), (0,)), ((), ()))
shape = jax.ShapeDtypeStruct


def call(kernel, name, args, ins, outs, scratch, mib, moved=0):
    args = [
        pltpu.with_memory_space_constraint(a, s.memory_space) if any(s is b for b in BOUND) else a
        for a, s in zip(args, ins)
    ]
    return pl.pallas_call(
        kernel,
        out_shape=tuple(
            s.memory_space(o.shape, o.dtype) if any(s is b for b in BOUND) else o for o, s in outs
        ),
        in_specs=ins,
        out_specs=tuple(s for _, s in outs),
        scratch_shapes=scratch,
        compiler_params=pltpu.CompilerParams(vmem_limit_bytes=mib * 1024 * 1024),
        cost_estimate=pl.CostEstimate(flops=100 * moved, bytes_accessed=moved, transcendentals=0),
        name=name,
    )(*args)


def copies(pairs, sems, first=0):
    return [
        pltpu.make_async_copy(source, to, sems.at[first + j]) for j, (source, to) in enumerate(pairs)
    ]


def start(group):
    for copy in group:
        copy.start()


def wait(group):
    for copy in group:
        copy.wait()


def iota(shape, axis):
    return lax.broadcasted_iota(jnp.int32, shape, axis)


def swap(rows, outer):
    at = iota((rows, rows), 0)
    source = (at % outer) * (rows // outer) + at // outer
    return (iota((rows, rows), 1) == source).astype(BF16)


def turn(x):
    return pltpu.roll(x, LANES // 2, 1)


def halves(pair):
    low = iota((pair.shape[0], LANES), 1) < LANES // 2
    one, two, three = (pair[:, j * LANES : (j + 1) * LANES] for j in range(3))
    two_turned, three_turned = turn(two), turn(three)
    zero = jnp.zeros_like(two)
    return (
        (one, jnp.where(low, two, zero)),
        (jnp.where(low, two_turned, three_turned), jnp.where(low, three_turned, zero)),
    )


def spread(source_ref, scratch, rows, count, late=None):
    size = rows * count
    for j in range(0, count, 2):
        pair = source_ref[:, j * TILE : (j + 2) * TILE].astype(F32)
        if late is not None:
            pair = jnp.where(late, pair[rows:], pair[:rows])
        for k, parts in enumerate(halves(pair)):
            for side, part in enumerate(parts):
                scratch[pl.ds(side * size + j + k, rows, stride=count), :] = part


def gather_sides(scratch, y_ref, blocks):
    size = blocks * RHS
    low = iota((blocks, LANES), 1) < LANES // 2
    for h in range(0, RHS, 2):
        one, two, three, four = (
            scratch[pl.ds(side * size + h + k, blocks, stride=RHS), :]
            for k in range(2)
            for side in range(2)
        )
        three, four = turn(three), turn(four)
        pair = (one, jnp.where(low, two, three), jnp.where(low, three, four))
        for j in range(3):
            at = h * TILE + j * LANES
            y_ref[:, at : at + LANES] = pair[j].astype(BF16)


def join(scratch, size):
    return jnp.concatenate(
        [scratch[side * size : (side + 1) * size, :].astype(BF16) for side in range(2)], axis=1
    )


def project(fields, basis_ref, coef_s):
    cols = GROUP * RANK
    lane = iota((RHS, LANES), 1) // RANK
    crosses = [
        lax.dot_general(
            field, basis_ref[g * cols : (g + 1) * cols, :], NT, preferred_element_type=F32
        )
        for g, field in enumerate(fields)
    ]
    for g, cross in enumerate(crosses):
        for half in range(GROUP // SIDE):
            out = None
            for j in range(SIDE):
                at = (half * SIDE + j) * RHS
                part = cross[at : at + RHS, half * LANES : (half + 1) * LANES]
                out = part if out is None else jnp.where(lane == j, part, out)
            at = (g * (GROUP // SIDE) + half) * RHS
            for j in range(coef_s.shape[0]):
                coef_s[j, at : at + RHS, :] = out.astype(BF16)


def opening_kernel(
    v_hbm, b_hbm, lo_ref, hi_ref, basis_ref, coef_ref, v_s, b_s, f_s, sems
):
    gets = copies(((v_hbm, v_s), (b_hbm, b_s)), sems)
    start(gets)
    blocks = v_s.shape[0]
    rows = blocks * RHS
    gets[0].wait()
    spread(v_s, f_s, blocks, RHS)
    field = join(f_s, rows)
    rim = RIM * RHS
    lo_ref[...] = field[:rim]
    hi_ref[...] = field[rim:]
    order = swap(blocks * blocks, blocks)
    gets[1].wait()
    for a in range(0, RANK, blocks):
        stack = []
        for p in range(a, a + blocks, 2):
            pair = b_s[:, p * TILE : (p + 2) * TILE]
            stack += [jnp.concatenate(parts, axis=1) for parts in halves(pair)]
        out = jnp.concatenate(stack, axis=0)
        out = lax.dot_general(order, out, NN, preferred_element_type=F32).astype(BF16)
        for i in range(blocks):
            basis_ref[i * RANK + a : i * RANK + a + blocks, :] = out[i * blocks : (i + 1) * blocks]
    project((field[:rim], field[rim:]), basis_ref, coef_ref)


def place(at_s, kind_s, e_s, p_s, unroll):
    blocks, slots = at_s.shape

    def one_block(i, _):
        row = pl.multiple_of(i * RHS, RHS)
        for k in range(slots):
            source = pl.multiple_of(at_s[i, k], RHS)
            column = pl.multiple_of(kind_s[i, k], WIDE)
            p_s[pl.ds(row, RHS), pl.ds(column, WIDE)] = e_s[pl.ds(source, RHS), :]
        return 0

    lax.fori_loop(0, blocks, one_block, 0, unroll=unroll)


def multiply(p_s, table_s, out_ref, chunk):
    size, columns = out_ref.shape[0], table_s.shape[1]
    out_ref[:, LANES:] = jnp.zeros((size, LANES), F32)

    def some_columns(n, total):
        at = pl.multiple_of(n * chunk, chunk)
        return total + lax.dot_general(
            p_s[:, pl.ds(at, chunk)], table_s[:, pl.ds(at, chunk)], NT, preferred_element_type=F32
        )

    total = jnp.zeros((size, TILE), F32)
    out_ref[:, :TILE] = lax.fori_loop(0, columns // chunk, some_columns, total)


def first_near_kernel(
    slabs, slab_blocks,
    count_hbm, src_hbm, type_hbm, far_hbm, tiles_hbm, coup_hbm, lo_ref, hi_ref, chip_ref, further_ref,
    near_ref, mat_ref, table_hbm, far_idx_ref, at_s, kind_s,
    count_s, src_s, type_s, far_s, tiles_s, coup_s, far_idx_s, at_v, kind_v,
    h_s, e_s, p_s, table_s, sems,
):
    gets = copies(
        (
            (count_hbm, count_s),
            (src_hbm, src_s),
            (type_hbm, type_s),
            (far_hbm, far_s),
            (coup_hbm, coup_s),
            (tiles_hbm, tiles_s),
        ),
        sems,
    )
    puts = copies(
        (
            (at_v, at_s),
            (kind_v, kind_s),
            (far_idx_s, far_idx_ref),
        ),
        sems,
        len(gets),
    )
    start(gets)
    types = tiles_s.shape[0]
    blocks, partners, _ = coup_s.shape
    deep = partners // SIDE
    size, rim = blocks * RHS, RIM * RHS
    me = lax.axis_index("slab")
    odd = me % 2 == 1

    p_s[:, : types * WIDE] = jnp.zeros((size, types * WIDE), BF16)
    e_s[:rim, :] = lo_ref[...]
    e_s[rim : 2 * rim, :] = hi_ref[...]
    for j, (ref, late) in enumerate(((chip_ref, odd), (further_ref, ~odd))):
        spread(ref, h_s, RIM, RHS, late)
        e_s[(2 + j) * rim : (3 + j) * rim, :] = join(h_s, rim)

    wait(gets[:4])
    source = src_s[...]
    step = (source // slab_blocks - me + slabs) % slabs
    after = jnp.where(odd, 3 * RIM, 2 * RIM)
    before = jnp.where(odd, RIM, 2 * RIM)
    offset = jnp.where(step == 0, 0, jnp.where(step == 1, after, before))
    at_v[...] = (source % blocks + offset) * RHS
    row = iota(source.shape, 0)
    count = jnp.zeros(source.shape, jnp.int32)
    for i in range(blocks):
        count = jnp.where(row == i, count_s[i], count)
    kind_v[...] = jnp.where(iota(source.shape, 1) < count, type_s[...], types) * WIDE

    source = far_s[...] % slab_blocks
    group = iota(source.shape, 1) // deep
    turned = (group - source) & (SIDE - 1)
    far_idx_s[...] = (turned * (slab_blocks // SIDE) + source // SIDE) * RHS
    start(puts)

    lane = iota((deep, LANES), 1) // RANK
    order = swap(RANK * deep, RANK)
    gets[4].wait()

    def two_blocks(n, _):
        stacks = []
        for b in range(2):
            i = 2 * n + b
            stack = []
            for big in range(RANK // SIDE):
                x = coup_s[i, :, big * LANES : (big + 1) * LANES].astype(F32)
                parts = [x[j * deep : (j + 1) * deep] for j in range(SIDE)]
                turned = [
                    [p if r == 0 else pltpu.roll(p, r * RANK, 1) for r in range(SIDE)]
                    for p in parts
                ]
                for small in range(SIDE):
                    out = turned[0][-small % SIDE]
                    for j in range(1, SIDE):
                        out = jnp.where(lane == j, turned[j][(j - small) % SIDE], out)
                    stack.append(out)
            stacks.append(jnp.concatenate(stack, axis=0).astype(BF16))
        both = jnp.concatenate(stacks, axis=1)
        both = lax.dot_general(order, both, NN, preferred_element_type=F32).astype(BF16)
        for b in range(2):
            at = pl.multiple_of((2 * n + b) * RANK, RANK)
            for k in range(deep):
                part = both[k * RANK : (k + 1) * RANK, b * LANES : (b + 1) * LANES]
                mat_ref[pl.ds(at, RANK), k * LANES : (k + 1) * LANES] = part
        return 0

    lax.fori_loop(0, blocks // 2, two_blocks, 0, unroll=True)

    wait(puts[:2])
    place(at_s, kind_s, e_s, p_s, True)

    many = 16
    order = swap(many * many, many)
    gets[5].wait()

    low = iota((many, LANES), 1) < LANES // 2
    steps = STEPS
    each = TILE // steps
    put_table = [
        copies(((table_s.at[rows], table_hbm.at[rows]),), sems, 9 + n)
        for n, rows in enumerate(pl.ds(n * each, each) for n in range(steps))
    ]

    def some_rows(step, _):
        for n in range(each // many):
            at = pl.multiple_of(step * (each * TILE), LANES) + n * many * TILE
            for a in range(types // many):
                stack = []
                for d in range(0, many, 2):
                    one, two, three = (
                        tiles_s[a * many : (a + 1) * many, pl.ds(at + d * TILE + j * LANES, LANES)]
                        for j in range(3)
                    )
                    two_turned, three_turned = turn(two), turn(three)
                    stack.append(jnp.concatenate((one, two), axis=1))
                    mixed = jnp.where(low, two_turned, three_turned)
                    stack.append(jnp.concatenate((mixed, three_turned), axis=1))
                out = jnp.concatenate(stack, axis=0)
                out = lax.dot_general(order, out, NN, preferred_element_type=F32).astype(BF16)
                for t in range(many):
                    to = (a * many + t) * WIDE
                    row = pl.multiple_of(step * each + n * many, many)
                    table_s[pl.ds(row, many), to : to + WIDE] = out[t * many : (t + 1) * many]
        rows = pl.ds(pl.multiple_of(step * each, many), each)
        start(copies(((table_s.at[rows], table_hbm.at[rows]),), sems, 9 + step))
        return 0

    lax.fori_loop(0, steps, some_rows, 0)
    multiply(p_s, table_s, near_ref, table_s.shape[1] // 2)
    wait(puts[2:])
    for put in put_table:
        wait(put)


def give_kernel(lo_ref, hi_ref, table_hbm, y_hbm, table_ref, f_s, y_s, sems):
    gets = copies(((table_hbm, table_ref),), sems)
    put = copies(((y_s, y_hbm),), sems, 1)
    start(gets)
    rim = lo_ref.shape[0]
    for k, ref in enumerate((lo_ref, hi_ref)):
        for j in range(2):
            at = (2 * j + k) * rim
            f_s[at : at + rim, :] = ref[:, j * LANES : (j + 1) * LANES].astype(F32)
    gather_sides(f_s, y_s, y_s.shape[0])
    start(put)
    wait(gets + put)


def second_near_kernel(
    at_s, kind_s, lo_ref, hi_ref, chip_ref, further_ref, table_ref, near_ref, e_s, p_s
):
    rim, columns = RIM * RHS, table_ref.shape[1]
    for j, ref in enumerate((lo_ref, hi_ref, chip_ref, further_ref)):
        e_s[j * rim : (j + 1) * rim, :] = ref[...]
    p_s[:, :columns] = jnp.zeros((p_s.shape[0], columns), BF16)
    place(at_s, kind_s, e_s, p_s, True)
    multiply(p_s, table_ref, near_ref, columns)


def far_kernel(last, idx_s, got_ref, mat_ref, basis_ref, near_ref, *rest):
    if last:
        y_ref, turn_s, pick_s, sum_s = rest
    else:
        lo_ref, hi_ref, chip_ref, further_ref, coef_ref, turn_s, pick_s = rest
    blocks, partners = idx_s.shape
    deep = partners // SIDE
    peers, packed_rows, _ = got_ref.shape
    quarter = peers * packed_rows
    for j in range(peers):
        got = got_ref[j]
        for r in range(SIDE):
            at = r * quarter + j * packed_rows
            turn_s[at : at + packed_rows, :] = got if r == 0 else pltpu.roll(got, r * RANK, 1)
    lane = iota((RHS, LANES), 1) // RANK

    def one_block(i, _):
        row = pl.multiple_of(i * RHS, RHS)
        for k in range(deep):
            out = None
            for j in range(SIDE):
                at = pl.multiple_of(idx_s[i, j * deep + k], RHS)
                part = turn_s[pl.ds(at, RHS), :]
                out = part if out is None else jnp.where(lane == j, part, out)
            pick_s[pl.ds(row, RHS), k * LANES : (k + 1) * LANES] = out
        return 0

    lax.fori_loop(0, blocks, one_block, 0, unroll=True)
    size = blocks * RHS
    rows, cols = GROUP * RHS, GROUP * RANK
    own = iota((rows, cols), 0) // RHS == iota((rows, cols), 1) // RANK
    groups = range(blocks // GROUP)
    crosses = [
        lax.dot_general(
            pick_s[g * rows : (g + 1) * rows, :],
            mat_ref[g * cols : (g + 1) * cols, :],
            NT,
            preferred_element_type=F32,
        )
        for g in groups
    ]
    mixes = [jnp.where(own, cross, 0.0).astype(BF16) for cross in crosses]
    totals = [
        near_ref[g * rows : (g + 1) * rows, :]
        + lax.dot_general(
            mixes[g], basis_ref[g * cols : (g + 1) * cols, :], NN, preferred_element_type=F32
        )
        for g in groups
    ]
    if last:
        for g in groups:
            for j in range(2):
                at = j * size + g * rows
                sum_s[at : at + rows, :] = totals[g][:, j * LANES : (j + 1) * LANES]
    fields = [total.astype(BF16) for total in totals]
    if last:
        gather_sides(sum_s, y_ref, blocks)
    else:
        project(fields, basis_ref, coef_ref)
        lo_ref[...], hi_ref[...] = lo, hi = fields
        odd = lax.axis_index("slab") % 2 == 1
        chip_ref[...] = jnp.where(odd, lo, hi)
        further_ref[...] = jnp.where(odd, hi, lo)


def opening(peers, vectors, bases):
    blocks = vectors.shape[0]
    rows, ranks, rim = blocks * RHS, blocks * RANK, RIM * RHS
    field = (shape((rim, WIDE), BF16), VMEM)
    coef = (peers, rows // SIDE, LANES)
    return call(
        opening_kernel, "opening", (vectors, bases), [HBM] * 2,
        [field, field, (shape((ranks, WIDE), BF16), VMEM), (shape(coef, BF16), VMEM)],
        [
            pltpu.VMEM(vectors.shape, BF16),
            pltpu.VMEM(bases.shape, BF16),
            pltpu.VMEM((2 * rows, LANES), F32),
            pltpu.SemaphoreType.DMA((2,)),
        ],
        8,
    )


def first_near(
    slabs, peers, near_count, near_src, near_type, far_src, tiles, coupling, lo, hi, chip, further
):
    blocks, partners, _ = coupling.shape
    rows, rim = blocks * RHS, RIM * RHS
    types = tiles.shape[0]
    table = (TILE, types * WIDE)
    slots = (near_src.shape, jnp.int32)
    picks = (far_src.shape, jnp.int32)
    return call(
        functools.partial(first_near_kernel, slabs, blocks * peers), "first_near",
        (near_count, near_src, near_type, far_src, tiles, coupling, lo, hi, chip, further),
        [HBM] * 6 + [VMEM] * 4,
        [
            (shape((rows, WIDE), F32), VMEM),
            (shape((blocks * RANK, partners * RANK), BF16), VMEM),
            (shape(table, BF16), HBM),
            (shape(*picks), SMEM),
            (shape(*slots), SMEM),
            (shape(*slots), SMEM),
        ],
        [
            pltpu.SMEM(near_count.shape, jnp.int32),
            pltpu.VMEM(*slots),
            pltpu.VMEM(*slots),
            pltpu.VMEM(*picks),
            pltpu.VMEM(tiles.shape, BF16),
            pltpu.VMEM(coupling.shape, BF16),
            pltpu.VMEM(*picks),
            pltpu.VMEM(*slots),
            pltpu.VMEM(*slots),
            pltpu.VMEM((2 * rim, LANES), F32),
            pltpu.VMEM((4 * rim, WIDE), BF16),
            pltpu.VMEM((rows, (types + 1) * WIDE), BF16),
            pltpu.VMEM(table, BF16),
            pltpu.SemaphoreType.DMA((9 + STEPS,)),
        ],
        20, LONG,
    )


def give(lo, hi, table):
    rows = 2 * lo.shape[0]
    y = (rows // RHS, RHS * TILE)
    return call(
        give_kernel, "give", (lo, hi, table), [VMEM] * 2 + [HBM],
        [(shape(y, BF16), HBM), (shape(table.shape, BF16), KEPT)],
        [
            pltpu.VMEM((2 * rows, LANES), F32),
            pltpu.VMEM(y, BF16),
            pltpu.SemaphoreType.DMA((2,)),
        ],
        4, 12_000_000,
    )


def second_near(at, kind, lo, hi, chip, further, table):
    rows = 2 * lo.shape[0]
    return call(
        second_near_kernel, "second_near", (at, kind, lo, hi, chip, further, table),
        [SMEM] * 2 + [VMEM] * 4 + [KEPT],
        [(shape((rows, WIDE), F32), VMEM)],
        [
            pltpu.VMEM((2 * rows, WIDE), BF16),
            pltpu.VMEM((rows, table.shape[1] + WIDE), BF16),
        ],
        8, 12_000_000,
    )[0]


def far(last, idx, got, mat, basis, near_term):
    rows = near_term.shape[0]
    peers, packed, _ = got.shape
    scratch = [
        pltpu.VMEM((SIDE * peers * packed, LANES), BF16),
        pltpu.VMEM((rows, mat.shape[1]), BF16),
    ]
    if last:
        outs = [(shape((rows // RHS, RHS * TILE), BF16), VMEM)]
        scratch.append(pltpu.VMEM((2 * rows, LANES), F32))
    else:
        outs = [(shape((rows // 2, WIDE), BF16), VMEM)] * 4 + [(shape(got.shape, BF16), VMEM)]
    return call(
        functools.partial(far_kernel, last), "far_last" if last else "far",
        (idx, got, mat, basis, near_term), [SMEM] + [VMEM] * 4, outs, scratch, 8,
    )


def per_device(vectors, tiles, near_src, near_type, near_count, bases, far_src, coupling):
    slabs, peers = lax.axis_size("slab"), lax.axis_size("grp")
    chips = [(i, i ^ 1) for i in range(slabs)]
    between = [(i, (i + 1 if i % 2 else i - 1) % slabs) for i in range(slabs)]

    def halo(chip, further):
        return lax.ppermute(chip, "slab", chips), lax.ppermute(further, "slab", between)

    def exchange(coef):
        return lax.all_to_all(coef, "grp", 0, 0, tiled=True)

    chip, further = halo(vectors, vectors)
    lo, hi, basis, coef = opening(peers, vectors, bases)
    got = exchange(coef)
    near_term, mat, table, idx, at, kind = first_near(
        slabs, peers, near_count, near_src, near_type, far_src, tiles, coupling, lo, hi, chip, further
    )
    lo, hi, chip, further, coef = far(False, idx, got, mat, basis, near_term)
    got = exchange(coef)
    chip, further = halo(chip, further)
    first, table = give(lo, hi, table)
    near_term = second_near(at, kind, lo, hi, chip, further, table)
    (second,) = far(True, idx, got, mat, basis, near_term)
    return (first, second)


def solution(mesh):
    in_specs = (
        P(("slab", "grp"), None),
        P(),
        P(("slab", "grp"), None),
        P(("slab", "grp"), None),
        P(("slab", "grp")),
        P(("slab", "grp"), None),
        P(("slab", "grp"), None),
        P(("slab", "grp"), None, None),
    )
    out_specs = (P(("slab", "grp"), None), P(("slab", "grp"), None))
    return jax.shard_map(
        per_device, mesh=mesh, in_specs=in_specs, out_specs=out_specs, check_vma=False
    )
```

```python
import functools

import jax
import jax.numpy as jnp
from jax import lax
from jax.experimental import pallas as pl
from jax.experimental.pallas import tpu as pltpu
from jax.sharding import PartitionSpec as P

TILE = 192
RHS = 16
RANK = 32
RIM = 8
LANES = 128
WIDE = 256
GROUP = 8
LONG = 100_000_000
STEPS = 2
SIDE = LANES // RANK

VMEM = pl.BlockSpec(memory_space=pltpu.VMEM)
SMEM = pl.BlockSpec(memory_space=pltpu.SMEM)
HBM = pl.BlockSpec(memory_space=pltpu.HBM)
KEPT = pl.BlockSpec(memory_space=pltpu.VMEM)
BOUND = (HBM, SMEM, KEPT)
F32 = jnp.float32
BF16 = jnp.bfloat16
NT = (((1,), (1,)), ((), ()))
NN = (((1,), (0,)), ((), ()))
shape = jax.ShapeDtypeStruct


def call(kernel, name, args, ins, outs, scratch, mib, moved=0):
    args = [
        pltpu.with_memory_space_constraint(a, s.memory_space) if any(s is b for b in BOUND) else a
        for a, s in zip(args, ins)
    ]
    return pl.pallas_call(
        kernel,
        out_shape=tuple(
            s.memory_space(o.shape, o.dtype) if any(s is b for b in BOUND) else o for o, s in outs
        ),
        in_specs=ins,
        out_specs=tuple(s for _, s in outs),
        scratch_shapes=scratch,
        compiler_params=pltpu.CompilerParams(vmem_limit_bytes=mib * 1024 * 1024),
        cost_estimate=pl.CostEstimate(flops=100 * moved, bytes_accessed=moved, transcendentals=0),
        name=name,
    )(*args)


def copies(pairs, sems, first=0):
    return [
        pltpu.make_async_copy(source, to, sems.at[first + j]) for j, (source, to) in enumerate(pairs)
    ]


def start(group):
    for copy in group:
        copy.start()


def wait(group):
    for copy in group:
        copy.wait()


def iota(shape, axis):
    return lax.broadcasted_iota(jnp.int32, shape, axis)


def swap(rows, outer):
    at = iota((rows, rows), 0)
    source = (at % outer) * (rows // outer) + at // outer
    return (iota((rows, rows), 1) == source).astype(BF16)


def turn(x):
    return pltpu.roll(x, LANES // 2, 1)


def halves(pair):
    low = iota((pair.shape[0], LANES), 1) < LANES // 2
    one, two, three = (pair[:, j * LANES : (j + 1) * LANES] for j in range(3))
    two_turned, three_turned = turn(two), turn(three)
    zero = jnp.zeros_like(two)
    return (
        (one, jnp.where(low, two, zero)),
        (jnp.where(low, two_turned, three_turned), jnp.where(low, three_turned, zero)),
    )


def spread(source_ref, scratch, rows, count, late=None):
    size = rows * count
    for j in range(0, count, 2):
        pair = source_ref[:, j * TILE : (j + 2) * TILE].astype(F32)
        if late is not None:
            pair = jnp.where(late, pair[rows:], pair[:rows])
        for k, parts in enumerate(halves(pair)):
            for side, part in enumerate(parts):
                scratch[pl.ds(side * size + j + k, rows, stride=count), :] = part


def gather_sides(scratch, y_ref, blocks):
    size = blocks * RHS
    low = iota((blocks, LANES), 1) < LANES // 2
    for h in range(0, RHS, 2):
        one, two, three, four = (
            scratch[pl.ds(side * size + h + k, blocks, stride=RHS), :]
            for k in range(2)
            for side in range(2)
        )
        three, four = turn(three), turn(four)
        pair = (one, jnp.where(low, two, three), jnp.where(low, three, four))
        for j in range(3):
            at = h * TILE + j * LANES
            y_ref[:, at : at + LANES] = pair[j].astype(BF16)


def join(scratch, size):
    return jnp.concatenate(
        [scratch[side * size : (side + 1) * size, :].astype(BF16) for side in range(2)], axis=1
    )


def project(fields, basis_ref, coef_s):
    cols = GROUP * RANK
    lane = iota((RHS, LANES), 1) // RANK
    crosses = [
        lax.dot_general(
            field, basis_ref[g * cols : (g + 1) * cols, :], NT, preferred_element_type=F32
        )
        for g, field in enumerate(fields)
    ]
    for g, cross in enumerate(crosses):
        for half in range(GROUP // SIDE):
            out = None
            for j in range(SIDE):
                at = (half * SIDE + j) * RHS
                part = cross[at : at + RHS, half * LANES : (half + 1) * LANES]
                out = part if out is None else jnp.where(lane == j, part, out)
            at = (g * (GROUP // SIDE) + half) * RHS
            for j in range(coef_s.shape[0]):
                coef_s[j, at : at + RHS, :] = out.astype(BF16)


def opening_kernel(
    v_hbm, b_hbm, lo_ref, hi_ref, basis_ref, coef_ref, v_s, b_s, f_s, sems
):
    gets = copies(((v_hbm, v_s), (b_hbm, b_s)), sems)
    start(gets)
    blocks = v_s.shape[0]
    rows = blocks * RHS
    gets[0].wait()
    spread(v_s, f_s, blocks, RHS)
    field = join(f_s, rows)
    rim = RIM * RHS
    lo_ref[...] = field[:rim]
    hi_ref[...] = field[rim:]
    order = swap(blocks * blocks, blocks)
    gets[1].wait()
    for a in range(0, RANK, blocks):
        stack = []
        for p in range(a, a + blocks, 2):
            pair = b_s[:, p * TILE : (p + 2) * TILE]
            stack += [jnp.concatenate(parts, axis=1) for parts in halves(pair)]
        out = jnp.concatenate(stack, axis=0)
        out = lax.dot_general(order, out, NN, preferred_element_type=F32).astype(BF16)
        for i in range(blocks):
            basis_ref[i * RANK + a : i * RANK + a + blocks, :] = out[i * blocks : (i + 1) * blocks]
    project((field[:rim], field[rim:]), basis_ref, coef_ref)


def place(at_s, kind_s, e_s, p_s, unroll):
    blocks, slots = at_s.shape

    def one_block(i, _):
        row = pl.multiple_of(i * RHS, RHS)
        for k in range(slots):
            source = pl.multiple_of(at_s[i, k], RHS)
            column = pl.multiple_of(kind_s[i, k], WIDE)
            p_s[pl.ds(row, RHS), pl.ds(column, WIDE)] = e_s[pl.ds(source, RHS), :]
        return 0

    lax.fori_loop(0, blocks, one_block, 0, unroll=unroll)


def multiply(p_s, table_s, out_ref, chunk):
    size, columns = out_ref.shape[0], table_s.shape[1]
    out_ref[:, LANES:] = jnp.zeros((size, LANES), F32)

    def some_columns(n, total):
        at = pl.multiple_of(n * chunk, chunk)
        return total + lax.dot_general(
            p_s[:, pl.ds(at, chunk)], table_s[:, pl.ds(at, chunk)], NT, preferred_element_type=F32
        )

    total = jnp.zeros((size, TILE), F32)
    out_ref[:, :TILE] = lax.fori_loop(0, columns // chunk, some_columns, total)


def first_near_kernel(
    slabs, slab_blocks,
    count_hbm, src_hbm, type_hbm, far_hbm, tiles_hbm, coup_hbm, lo_ref, hi_ref, chip_ref, further_ref,
    near_ref, mat_ref, table_hbm, far_idx_ref, at_s, kind_s,
    count_s, src_s, type_s, far_s, tiles_s, coup_s, far_idx_s, at_v, kind_v,
    h_s, e_s, p_s, table_s, sems,
):
    gets = copies(
        (
            (count_hbm, count_s),
            (src_hbm, src_s),
            (type_hbm, type_s),
            (far_hbm, far_s),
            (coup_hbm, coup_s),
            (tiles_hbm, tiles_s),
        ),
        sems,
    )
    puts = copies(
        (
            (at_v, at_s),
            (kind_v, kind_s),
            (far_idx_s, far_idx_ref),
        ),
        sems,
        len(gets),
    )
    start(gets)
    types = tiles_s.shape[0]
    blocks, partners, _ = coup_s.shape
    deep = partners // SIDE
    size, rim = blocks * RHS, RIM * RHS
    me = lax.axis_index("slab")
    odd = me % 2 == 1

    p_s[:, : types * WIDE] = jnp.zeros((size, types * WIDE), BF16)
    e_s[:rim, :] = lo_ref[...]
    e_s[rim : 2 * rim, :] = hi_ref[...]
    for j, (ref, late) in enumerate(((chip_ref, odd), (further_ref, ~odd))):
        spread(ref, h_s, RIM, RHS, late)
        e_s[(2 + j) * rim : (3 + j) * rim, :] = join(h_s, rim)

    wait(gets[:4])
    source = src_s[...]
    step = (source // slab_blocks - me + slabs) % slabs
    after = jnp.where(odd, 3 * RIM, 2 * RIM)
    before = jnp.where(odd, RIM, 2 * RIM)
    offset = jnp.where(step == 0, 0, jnp.where(step == 1, after, before))
    at_v[...] = (source % blocks + offset) * RHS
    row = iota(source.shape, 0)
    count = jnp.zeros(source.shape, jnp.int32)
    for i in range(blocks):
        count = jnp.where(row == i, count_s[i], count)
    kind_v[...] = jnp.where(iota(source.shape, 1) < count, type_s[...], types) * WIDE

    source = far_s[...] % slab_blocks
    group = iota(source.shape, 1) // deep
    turned = (group - source) & (SIDE - 1)
    far_idx_s[...] = (turned * (slab_blocks // SIDE) + source // SIDE) * RHS
    start(puts)

    lane = iota((deep, LANES), 1) // RANK
    order = swap(RANK * deep, RANK)
    gets[4].wait()

    def two_blocks(n, _):
        stacks = []
        for b in range(2):
            i = 2 * n + b
            stack = []
            for big in range(RANK // SIDE):
                x = coup_s[i, :, big * LANES : (big + 1) * LANES].astype(F32)
                parts = [x[j * deep : (j + 1) * deep] for j in range(SIDE)]
                turned = [
                    [p if r == 0 else pltpu.roll(p, r * RANK, 1) for r in range(SIDE)]
                    for p in parts
                ]
                for small in range(SIDE):
                    out = turned[0][-small % SIDE]
                    for j in range(1, SIDE):
                        out = jnp.where(lane == j, turned[j][(j - small) % SIDE], out)
                    stack.append(out)
            stacks.append(jnp.concatenate(stack, axis=0).astype(BF16))
        both = jnp.concatenate(stacks, axis=1)
        both = lax.dot_general(order, both, NN, preferred_element_type=F32).astype(BF16)
        for b in range(2):
            at = pl.multiple_of((2 * n + b) * RANK, RANK)
            for k in range(deep):
                part = both[k * RANK : (k + 1) * RANK, b * LANES : (b + 1) * LANES]
                mat_ref[pl.ds(at, RANK), k * LANES : (k + 1) * LANES] = part
        return 0

    lax.fori_loop(0, blocks // 2, two_blocks, 0, unroll=True)

    wait(puts[:2])
    place(at_s, kind_s, e_s, p_s, True)

    many = 16
    order = swap(many * many, many)
    gets[5].wait()

    low = iota((many, LANES), 1) < LANES // 2
    steps = STEPS
    each = TILE // steps
    put_table = [
        copies(((table_s.at[rows], table_hbm.at[rows]),), sems, 9 + n)
        for n, rows in enumerate(pl.ds(n * each, each) for n in range(steps))
    ]

    def some_rows(step, _):
        for n in range(each // many):
            at = pl.multiple_of(step * (each * TILE), LANES) + n * many * TILE
            for a in range(types // many):
                stack = []
                for d in range(0, many, 2):
                    one, two, three = (
                        tiles_s[a * many : (a + 1) * many, pl.ds(at + d * TILE + j * LANES, LANES)]
                        for j in range(3)
                    )
                    two_turned, three_turned = turn(two), turn(three)
                    stack.append(jnp.concatenate((one, two), axis=1))
                    mixed = jnp.where(low, two_turned, three_turned)
                    stack.append(jnp.concatenate((mixed, three_turned), axis=1))
                out = jnp.concatenate(stack, axis=0)
                out = lax.dot_general(order, out, NN, preferred_element_type=F32).astype(BF16)
                for t in range(many):
                    to = (a * many + t) * WIDE
                    row = pl.multiple_of(step * each + n * many, many)
                    table_s[pl.ds(row, many), to : to + WIDE] = out[t * many : (t + 1) * many]
        rows = pl.ds(pl.multiple_of(step * each, many), each)
        start(copies(((table_s.at[rows], table_hbm.at[rows]),), sems, 9 + step))
        return 0

    lax.fori_loop(0, steps, some_rows, 0)
    multiply(p_s, table_s, near_ref, table_s.shape[1] // 2)
    wait(puts[2:])
    for put in put_table:
        wait(put)


def give_kernel(lo_ref, hi_ref, table_hbm, y_hbm, table_ref, f_s, y_s, sems):
    gets = copies(((table_hbm, table_ref),), sems)
    put = copies(((y_s, y_hbm),), sems, 1)
    start(gets)
    rim = lo_ref.shape[0]
    for k, ref in enumerate((lo_ref, hi_ref)):
        for j in range(2):
            at = (2 * j + k) * rim
            f_s[at : at + rim, :] = ref[:, j * LANES : (j + 1) * LANES].astype(F32)
    gather_sides(f_s, y_s, y_s.shape[0])
    start(put)
    wait(gets + put)


def second_near_kernel(
    at_s, kind_s, lo_ref, hi_ref, further_ref, chip_ref, table_ref, near_ref, e_s, p_s
):
    rim, columns = RIM * RHS, table_ref.shape[1]
    for j, ref in enumerate((lo_ref, hi_ref, chip_ref, further_ref)):
        e_s[j * rim : (j + 1) * rim, :] = ref[...]
    p_s[:, :columns] = jnp.zeros((p_s.shape[0], columns), BF16)
    place(at_s, kind_s, e_s, p_s, True)
    multiply(p_s, table_ref, near_ref, columns)


def far_kernel(last, idx_s, got_ref, mat_ref, basis_ref, near_ref, *rest):
    if last:
        y_ref, turn_s, pick_s, sum_s = rest
    else:
        lo_ref, hi_ref, chip_ref, further_ref, coef_ref, turn_s, pick_s = rest
    blocks, partners = idx_s.shape
    deep = partners // SIDE
    peers, packed_rows, _ = got_ref.shape
    quarter = peers * packed_rows
    for j in range(peers):
        got = got_ref[j]
        for r in range(SIDE):
            at = r * quarter + j * packed_rows
            turn_s[at : at + packed_rows, :] = got if r == 0 else pltpu.roll(got, r * RANK, 1)
    lane = iota((RHS, LANES), 1) // RANK

    def one_block(i, _):
        row = pl.multiple_of(i * RHS, RHS)
        for k in range(deep):
            out = None
            for j in range(SIDE):
                at = pl.multiple_of(idx_s[i, j * deep + k], RHS)
                part = turn_s[pl.ds(at, RHS), :]
                out = part if out is None else jnp.where(lane == j, part, out)
            pick_s[pl.ds(row, RHS), k * LANES : (k + 1) * LANES] = out
        return 0

    lax.fori_loop(0, blocks, one_block, 0, unroll=True)
    size = blocks * RHS
    rows, cols = GROUP * RHS, GROUP * RANK
    own = iota((rows, cols), 0) // RHS == iota((rows, cols), 1) // RANK
    groups = range(blocks // GROUP)
    crosses = [
        lax.dot_general(
            pick_s[g * rows : (g + 1) * rows, :],
            mat_ref[g * cols : (g + 1) * cols, :],
            NT,
            preferred_element_type=F32,
        )
        for g in groups
    ]
    mixes = [jnp.where(own, cross, 0.0).astype(BF16) for cross in crosses]
    totals = [
        near_ref[g * rows : (g + 1) * rows, :]
        + lax.dot_general(
            mixes[g], basis_ref[g * cols : (g + 1) * cols, :], NN, preferred_element_type=F32
        )
        for g in groups
    ]
    if last:
        for g in groups:
            for j in range(2):
                at = j * size + g * rows
                sum_s[at : at + rows, :] = totals[g][:, j * LANES : (j + 1) * LANES]
    fields = [total.astype(BF16) for total in totals]
    if last:
        gather_sides(sum_s, y_ref, blocks)
    else:
        project(fields, basis_ref, coef_ref)
        lo_ref[...], hi_ref[...] = lo, hi = fields
        odd = lax.axis_index("slab") % 2 == 1
        chip_ref[...] = jnp.where(odd, lo, hi)
        further_ref[...] = jnp.where(odd, hi, lo)


def opening(peers, vectors, bases):
    blocks = vectors.shape[0]
    rows, ranks, rim = blocks * RHS, blocks * RANK, RIM * RHS
    field = (shape((rim, WIDE), BF16), VMEM)
    coef = (peers, rows // SIDE, LANES)
    return call(
        opening_kernel, "opening", (vectors, bases), [HBM] * 2,
        [field, field, (shape((ranks, WIDE), BF16), VMEM), (shape(coef, BF16), VMEM)],
        [
            pltpu.VMEM(vectors.shape, BF16),
            pltpu.VMEM(bases.shape, BF16),
            pltpu.VMEM((2 * rows, LANES), F32),
            pltpu.SemaphoreType.DMA((2,)),
        ],
        8,
    )


def first_near(
    slabs, peers, near_count, near_src, near_type, far_src, tiles, coupling, lo, hi, chip, further
):
    blocks, partners, _ = coupling.shape
    rows, rim = blocks * RHS, RIM * RHS
    types = tiles.shape[0]
    table = (TILE, types * WIDE)
    slots = (near_src.shape, jnp.int32)
    picks = (far_src.shape, jnp.int32)
    return call(
        functools.partial(first_near_kernel, slabs, blocks * peers), "first_near",
        (near_count, near_src, near_type, far_src, tiles, coupling, lo, hi, chip, further),
        [HBM] * 6 + [VMEM] * 4,
        [
            (shape((rows, WIDE), F32), VMEM),
            (shape((blocks * RANK, partners * RANK), BF16), VMEM),
            (shape(table, BF16), HBM),
            (shape(*picks), SMEM),
            (shape(*slots), SMEM),
            (shape(*slots), SMEM),
        ],
        [
            pltpu.SMEM(near_count.shape, jnp.int32),
            pltpu.VMEM(*slots),
            pltpu.VMEM(*slots),
            pltpu.VMEM(*picks),
            pltpu.VMEM(tiles.shape, BF16),
            pltpu.VMEM(coupling.shape, BF16),
            pltpu.VMEM(*picks),
            pltpu.VMEM(*slots),
            pltpu.VMEM(*slots),
            pltpu.VMEM((2 * rim, LANES), F32),
            pltpu.VMEM((4 * rim, WIDE), BF16),
            pltpu.VMEM((rows, (types + 1) * WIDE), BF16),
            pltpu.VMEM(table, BF16),
            pltpu.SemaphoreType.DMA((9 + STEPS,)),
        ],
        20, LONG,
    )


def give(lo, hi, table):
    rows = 2 * lo.shape[0]
    y = (rows // RHS, RHS * TILE)
    return call(
        give_kernel, "give", (lo, hi, table), [VMEM] * 2 + [HBM],
        [(shape(y, BF16), HBM), (shape(table.shape, BF16), KEPT)],
        [
            pltpu.VMEM((2 * rows, LANES), F32),
            pltpu.VMEM(y, BF16),
            pltpu.SemaphoreType.DMA((2,)),
        ],
        4, 12_000_000,
    )


def second_near(at, kind, lo, hi, chip, further, table):
    rows = 2 * lo.shape[0]
    return call(
        second_near_kernel, "second_near", (at, kind, lo, hi, further, chip, table),
        [SMEM] * 2 + [VMEM] * 4 + [KEPT],
        [(shape((rows, WIDE), F32), VMEM)],
        [
            pltpu.VMEM((2 * rows, WIDE), BF16),
            pltpu.VMEM((rows, table.shape[1] + WIDE), BF16),
        ],
        8, 12_000_000,
    )[0]


def far(last, idx, got, mat, basis, near_term):
    rows = near_term.shape[0]
    peers, packed, _ = got.shape
    scratch = [
        pltpu.VMEM((SIDE * peers * packed, LANES), BF16),
        pltpu.VMEM((rows, mat.shape[1]), BF16),
    ]
    if last:
        outs = [(shape((rows // RHS, RHS * TILE), BF16), VMEM)]
        scratch.append(pltpu.VMEM((2 * rows, LANES), F32))
    else:
        outs = [(shape((rows // 2, WIDE), BF16), VMEM)] * 4 + [(shape(got.shape, BF16), VMEM)]
    return call(
        functools.partial(far_kernel, last), "far_last" if last else "far",
        (idx, got, mat, basis, near_term), [SMEM] + [VMEM] * 4, outs, scratch, 8,
    )


def per_device(vectors, tiles, near_src, near_type, near_count, bases, far_src, coupling):
    slabs, peers = lax.axis_size("slab"), lax.axis_size("grp")
    chips = [(i, i ^ 1) for i in range(slabs)]
    between = [(i, (i + 1 if i % 2 else i - 1) % slabs) for i in range(slabs)]

    def halo(chip, further):
        return lax.ppermute(chip, "slab", chips), lax.ppermute(further, "slab", between)

    def exchange(coef):
        return lax.all_to_all(coef, "grp", 0, 0, tiled=True)

    chip, further = halo(vectors, vectors)
    lo, hi, basis, coef = opening(peers, vectors, bases)
    got = exchange(coef)
    near_term, mat, table, idx, at, kind = first_near(
        slabs, peers, near_count, near_src, near_type, far_src, tiles, coupling, lo, hi, chip, further
    )
    lo, hi, chip, further, coef = far(False, idx, got, mat, basis, near_term)
    got = exchange(coef)
    chip, further = halo(chip, further)
    first, table = give(lo, hi, table)
    near_term = second_near(at, kind, lo, hi, chip, further, table)
    (second,) = far(True, idx, got, mat, basis, near_term)
    return (first, second)


def solution(mesh):
    in_specs = (
        P(("slab", "grp"), None),
        P(),
        P(("slab", "grp"), None),
        P(("slab", "grp"), None),
        P(("slab", "grp")),
        P(("slab", "grp"), None),
        P(("slab", "grp"), None),
        P(("slab", "grp"), None, None),
    )
    out_specs = (P(("slab", "grp"), None), P(("slab", "grp"), None))
    return jax.shard_map(
        per_device, mesh=mesh, in_specs=in_specs, out_specs=out_specs, check_vma=False
    )
```

```python
import functools

import jax
import jax.numpy as jnp
from jax import lax
from jax.experimental import pallas as pl
from jax.experimental.pallas import tpu as pltpu
from jax.sharding import PartitionSpec as P

TILE = 192
RHS = 16
RANK = 32
RIM = 8
LANES = 128
WIDE = 256
GROUP = 8
LONG = 100_000_000
STEPS = 1
SIDE = LANES // RANK

VMEM = pl.BlockSpec(memory_space=pltpu.VMEM)
SMEM = pl.BlockSpec(memory_space=pltpu.SMEM)
HBM = pl.BlockSpec(memory_space=pltpu.HBM)
KEPT = pl.BlockSpec(memory_space=pltpu.VMEM)
BOUND = (HBM, SMEM, KEPT)
F32 = jnp.float32
BF16 = jnp.bfloat16
NT = (((1,), (1,)), ((), ()))
NN = (((1,), (0,)), ((), ()))
shape = jax.ShapeDtypeStruct


def call(kernel, name, args, ins, outs, scratch, mib, moved=0):
    args = [
        pltpu.with_memory_space_constraint(a, s.memory_space) if any(s is b for b in BOUND) else a
        for a, s in zip(args, ins)
    ]
    return pl.pallas_call(
        kernel,
        out_shape=tuple(
            s.memory_space(o.shape, o.dtype) if any(s is b for b in BOUND) else o for o, s in outs
        ),
        in_specs=ins,
        out_specs=tuple(s for _, s in outs),
        scratch_shapes=scratch,
        compiler_params=pltpu.CompilerParams(vmem_limit_bytes=mib * 1024 * 1024),
        cost_estimate=pl.CostEstimate(flops=100 * moved, bytes_accessed=moved, transcendentals=0),
        name=name,
    )(*args)


def copies(pairs, sems, first=0):
    return [
        pltpu.make_async_copy(source, to, sems.at[first + j]) for j, (source, to) in enumerate(pairs)
    ]


def start(group):
    for copy in group:
        copy.start()


def wait(group):
    for copy in group:
        copy.wait()


def iota(shape, axis):
    return lax.broadcasted_iota(jnp.int32, shape, axis)


def swap(rows, outer):
    at = iota((rows, rows), 0)
    source = (at % outer) * (rows // outer) + at // outer
    return (iota((rows, rows), 1) == source).astype(BF16)


def turn(x):
    return pltpu.roll(x, LANES // 2, 1)


def halves(pair):
    low = iota((pair.shape[0], LANES), 1) < LANES // 2
    one, two, three = (pair[:, j * LANES : (j + 1) * LANES] for j in range(3))
    two_turned, three_turned = turn(two), turn(three)
    zero = jnp.zeros_like(two)
    return (
        (one, jnp.where(low, two, zero)),
        (jnp.where(low, two_turned, three_turned), jnp.where(low, three_turned, zero)),
    )


def spread(source_ref, scratch, rows, count, late=None):
    size = rows * count
    for j in range(0, count, 2):
        pair = source_ref[:, j * TILE : (j + 2) * TILE].astype(F32)
        if late is not None:
            pair = jnp.where(late, pair[rows:], pair[:rows])
        for k, parts in enumerate(halves(pair)):
            for side, part in enumerate(parts):
                scratch[pl.ds(side * size + j + k, rows, stride=count), :] = part


def gather_sides(scratch, y_ref, blocks):
    size = blocks * RHS
    low = iota((blocks, LANES), 1) < LANES // 2
    for h in range(0, RHS, 2):
        one, two, three, four = (
            scratch[pl.ds(side * size + h + k, blocks, stride=RHS), :]
            for k in range(2)
            for side in range(2)
        )
        three, four = turn(three), turn(four)
        pair = (one, jnp.where(low, two, three), jnp.where(low, three, four))
        for j in range(3):
            at = h * TILE + j * LANES
            y_ref[:, at : at + LANES] = pair[j].astype(BF16)


def join(scratch, size):
    return jnp.concatenate(
        [scratch[side * size : (side + 1) * size, :].astype(BF16) for side in range(2)], axis=1
    )


def project(fields, basis_ref, coef_s):
    cols = GROUP * RANK
    lane = iota((RHS, LANES), 1) // RANK
    crosses = [
        lax.dot_general(
            field, basis_ref[g * cols : (g + 1) * cols, :], NT, preferred_element_type=F32
        )
        for g, field in enumerate(fields)
    ]
    for g, cross in enumerate(crosses):
        for half in range(GROUP // SIDE):
            out = None
            for j in range(SIDE):
                at = (half * SIDE + j) * RHS
                part = cross[at : at + RHS, half * LANES : (half + 1) * LANES]
                out = part if out is None else jnp.where(lane == j, part, out)
            at = (g * (GROUP // SIDE) + half) * RHS
            for j in range(coef_s.shape[0]):
                coef_s[j, at : at + RHS, :] = out.astype(BF16)


def opening_kernel(
    v_hbm, b_hbm, lo_ref, hi_ref, basis_ref, coef_ref, v_s, b_s, f_s, sems
):
    gets = copies(((v_hbm, v_s), (b_hbm, b_s)), sems)
    start(gets)
    blocks = v_s.shape[0]
    rows = blocks * RHS
    gets[0].wait()
    spread(v_s, f_s, blocks, RHS)
    field = join(f_s, rows)
    rim = RIM * RHS
    lo_ref[...] = field[:rim]
    hi_ref[...] = field[rim:]
    order = swap(blocks * blocks, blocks)
    gets[1].wait()
    for a in range(0, RANK, blocks):
        stack = []
        for p in range(a, a + blocks, 2):
            pair = b_s[:, p * TILE : (p + 2) * TILE]
            stack += [jnp.concatenate(parts, axis=1) for parts in halves(pair)]
        out = jnp.concatenate(stack, axis=0)
        out = lax.dot_general(order, out, NN, preferred_element_type=F32).astype(BF16)
        for i in range(blocks):
            basis_ref[i * RANK + a : i * RANK + a + blocks, :] = out[i * blocks : (i + 1) * blocks]
    project((field[:rim], field[rim:]), basis_ref, coef_ref)


def place(at_s, kind_s, e_s, p_s, unroll):
    blocks, slots = at_s.shape

    def one_block(i, _):
        row = pl.multiple_of(i * RHS, RHS)
        for k in range(slots):
            source = pl.multiple_of(at_s[i, k], RHS)
            column = pl.multiple_of(kind_s[i, k], WIDE)
            p_s[pl.ds(row, RHS), pl.ds(column, WIDE)] = e_s[pl.ds(source, RHS), :]
        return 0

    lax.fori_loop(0, blocks, one_block, 0, unroll=unroll)


def multiply(p_s, table_s, out_ref, chunk):
    size, columns = out_ref.shape[0], table_s.shape[1]
    out_ref[:, LANES:] = jnp.zeros((size, LANES), F32)

    def some_columns(n, total):
        at = pl.multiple_of(n * chunk, chunk)
        return total + lax.dot_general(
            p_s[:, pl.ds(at, chunk)], table_s[:, pl.ds(at, chunk)], NT, preferred_element_type=F32
        )

    total = jnp.zeros((size, TILE), F32)
    out_ref[:, :TILE] = lax.fori_loop(0, columns // chunk, some_columns, total)


def first_near_kernel(
    slabs, slab_blocks,
    count_hbm, src_hbm, type_hbm, far_hbm, tiles_hbm, coup_hbm, lo_ref, hi_ref, chip_ref, further_ref,
    near_ref, mat_ref, table_hbm, far_idx_ref, at_s, kind_s,
    count_s, src_s, type_s, far_s, tiles_s, coup_s, far_idx_s, at_v, kind_v,
    h_s, e_s, p_s, table_s, sems,
):
    gets = copies(
        (
            (count_hbm, count_s),
            (src_hbm, src_s),
            (type_hbm, type_s),
            (far_hbm, far_s),
            (coup_hbm, coup_s),
            (tiles_hbm, tiles_s),
        ),
        sems,
    )
    puts = copies(
        (
            (at_v, at_s),
            (kind_v, kind_s),
            (far_idx_s, far_idx_ref),
        ),
        sems,
        len(gets),
    )
    start(gets)
    types = tiles_s.shape[0]
    blocks, partners, _ = coup_s.shape
    deep = partners // SIDE
    size, rim = blocks * RHS, RIM * RHS
    me = lax.axis_index("slab")
    odd = me % 2 == 1

    p_s[:, : types * WIDE] = jnp.zeros((size, types * WIDE), BF16)
    e_s[:rim, :] = lo_ref[...]
    e_s[rim : 2 * rim, :] = hi_ref[...]
    for j, (ref, late) in enumerate(((chip_ref, odd), (further_ref, ~odd))):
        spread(ref, h_s, RIM, RHS, late)
        e_s[(2 + j) * rim : (3 + j) * rim, :] = join(h_s, rim)

    wait(gets[:4])
    source = src_s[...]
    step = (source // slab_blocks - me + slabs) % slabs
    after = jnp.where(odd, 3 * RIM, 2 * RIM)
    before = jnp.where(odd, RIM, 2 * RIM)
    offset = jnp.where(step == 0, 0, jnp.where(step == 1, after, before))
    at_v[...] = (source % blocks + offset) * RHS
    row = iota(source.shape, 0)
    count = jnp.zeros(source.shape, jnp.int32)
    for i in range(blocks):
        count = jnp.where(row == i, count_s[i], count)
    kind_v[...] = jnp.where(iota(source.shape, 1) < count, type_s[...], types) * WIDE

    source = far_s[...] % slab_blocks
    group = iota(source.shape, 1) // deep
    turned = (group - source) & (SIDE - 1)
    far_idx_s[...] = (turned * (slab_blocks // SIDE) + source // SIDE) * RHS
    start(puts)

    lane = iota((deep, LANES), 1) // RANK
    order = swap(RANK * deep, RANK)
    gets[4].wait()

    def two_blocks(n, _):
        stacks = []
        for b in range(2):
            i = 2 * n + b
            stack = []
            for big in range(RANK // SIDE):
                x = coup_s[i, :, big * LANES : (big + 1) * LANES].astype(F32)
                parts = [x[j * deep : (j + 1) * deep] for j in range(SIDE)]
                turned = [
                    [p if r == 0 else pltpu.roll(p, r * RANK, 1) for r in range(SIDE)]
                    for p in parts
                ]
                for small in range(SIDE):
                    out = turned[0][-small % SIDE]
                    for j in range(1, SIDE):
                        out = jnp.where(lane == j, turned[j][(j - small) % SIDE], out)
                    stack.append(out)
            stacks.append(jnp.concatenate(stack, axis=0).astype(BF16))
        both = jnp.concatenate(stacks, axis=1)
        both = lax.dot_general(order, both, NN, preferred_element_type=F32).astype(BF16)
        for b in range(2):
            at = pl.multiple_of((2 * n + b) * RANK, RANK)
            for k in range(deep):
                part = both[k * RANK : (k + 1) * RANK, b * LANES : (b + 1) * LANES]
                mat_ref[pl.ds(at, RANK), k * LANES : (k + 1) * LANES] = part
        return 0

    lax.fori_loop(0, blocks // 2, two_blocks, 0, unroll=True)

    wait(puts[:2])
    place(at_s, kind_s, e_s, p_s, True)

    many = 16
    order = swap(many * many, many)
    gets[5].wait()

    low = iota((many, LANES), 1) < LANES // 2
    steps = STEPS
    each = TILE // steps
    put_table = [
        copies(((table_s.at[rows], table_hbm.at[rows]),), sems, 9 + n)
        for n, rows in enumerate(pl.ds(n * each, each) for n in range(steps))
    ]

    def some_rows(step, _):
        for n in range(each // many):
            at = pl.multiple_of(step * (each * TILE), LANES) + n * many * TILE
            for a in range(types // many):
                stack = []
                for d in range(0, many, 2):
                    one, two, three = (
                        tiles_s[a * many : (a + 1) * many, pl.ds(at + d * TILE + j * LANES, LANES)]
                        for j in range(3)
                    )
                    two_turned, three_turned = turn(two), turn(three)
                    stack.append(jnp.concatenate((one, two), axis=1))
                    mixed = jnp.where(low, two_turned, three_turned)
                    stack.append(jnp.concatenate((mixed, three_turned), axis=1))
                out = jnp.concatenate(stack, axis=0)
                out = lax.dot_general(order, out, NN, preferred_element_type=F32).astype(BF16)
                for t in range(many):
                    to = (a * many + t) * WIDE
                    row = pl.multiple_of(step * each + n * many, many)
                    table_s[pl.ds(row, many), to : to + WIDE] = out[t * many : (t + 1) * many]
        rows = pl.ds(pl.multiple_of(step * each, many), each)
        start(copies(((table_s.at[rows], table_hbm.at[rows]),), sems, 9 + step))
        return 0

    lax.fori_loop(0, steps, some_rows, 0)
    multiply(p_s, table_s, near_ref, table_s.shape[1] // 2)
    wait(puts[2:])
    for put in put_table:
        wait(put)


def give_kernel(lo_ref, hi_ref, table_hbm, y_hbm, table_ref, f_s, y_s, sems):
    gets = copies(((table_hbm, table_ref),), sems)
    put = copies(((y_s, y_hbm),), sems, 1)
    start(gets)
    rim = lo_ref.shape[0]
    for k, ref in enumerate((lo_ref, hi_ref)):
        for j in range(2):
            at = (2 * j + k) * rim
            f_s[at : at + rim, :] = ref[:, j * LANES : (j + 1) * LANES].astype(F32)
    gather_sides(f_s, y_s, y_s.shape[0])
    start(put)
    wait(gets + put)


def second_near_kernel(
    at_s, kind_s, lo_ref, hi_ref, further_ref, chip_ref, table_ref, near_ref, e_s, p_s
):
    rim, columns = RIM * RHS, table_ref.shape[1]
    for j, ref in enumerate((lo_ref, hi_ref, chip_ref, further_ref)):
        e_s[j * rim : (j + 1) * rim, :] = ref[...]
    p_s[:, :columns] = jnp.zeros((p_s.shape[0], columns), BF16)
    place(at_s, kind_s, e_s, p_s, True)
    multiply(p_s, table_ref, near_ref, columns)


def far_kernel(last, idx_s, got_ref, mat_ref, basis_ref, near_ref, *rest):
    if last:
        y_ref, turn_s, pick_s, sum_s = rest
    else:
        lo_ref, hi_ref, chip_ref, further_ref, coef_ref, turn_s, pick_s = rest
    blocks, partners = idx_s.shape
    deep = partners // SIDE
    peers, packed_rows, _ = got_ref.shape
    quarter = peers * packed_rows
    for j in range(peers):
        got = got_ref[j]
        for r in range(SIDE):
            at = r * quarter + j * packed_rows
            turn_s[at : at + packed_rows, :] = got if r == 0 else pltpu.roll(got, r * RANK, 1)
    lane = iota((RHS, LANES), 1) // RANK

    def one_block(i, _):
        row = pl.multiple_of(i * RHS, RHS)
        for k in range(deep):
            out = None
            for j in range(SIDE):
                at = pl.multiple_of(idx_s[i, j * deep + k], RHS)
                part = turn_s[pl.ds(at, RHS), :]
                out = part if out is None else jnp.where(lane == j, part, out)
            pick_s[pl.ds(row, RHS), k * LANES : (k + 1) * LANES] = out
        return 0

    lax.fori_loop(0, blocks, one_block, 0, unroll=True)
    size = blocks * RHS
    rows, cols = GROUP * RHS, GROUP * RANK
    own = iota((rows, cols), 0) // RHS == iota((rows, cols), 1) // RANK
    groups = range(blocks // GROUP)
    crosses = [
        lax.dot_general(
            pick_s[g * rows : (g + 1) * rows, :],
            mat_ref[g * cols : (g + 1) * cols, :],
            NT,
            preferred_element_type=F32,
        )
        for g in groups
    ]
    mixes = [jnp.where(own, cross, 0.0).astype(BF16) for cross in crosses]
    totals = [
        near_ref[g * rows : (g + 1) * rows, :]
        + lax.dot_general(
            mixes[g], basis_ref[g * cols : (g + 1) * cols, :], NN, preferred_element_type=F32
        )
        for g in groups
    ]
    if last:
        for g in groups:
            for j in range(2):
                at = j * size + g * rows
                sum_s[at : at + rows, :] = totals[g][:, j * LANES : (j + 1) * LANES]
    fields = [total.astype(BF16) for total in totals]
    if last:
        gather_sides(sum_s, y_ref, blocks)
    else:
        project(fields, basis_ref, coef_ref)
        lo_ref[...], hi_ref[...] = lo, hi = fields
        odd = lax.axis_index("slab") % 2 == 1
        chip_ref[...] = jnp.where(odd, lo, hi)
        further_ref[...] = jnp.where(odd, hi, lo)


def opening(peers, vectors, bases):
    blocks = vectors.shape[0]
    rows, ranks, rim = blocks * RHS, blocks * RANK, RIM * RHS
    field = (shape((rim, WIDE), BF16), VMEM)
    coef = (peers, rows // SIDE, LANES)
    return call(
        opening_kernel, "opening", (vectors, bases), [HBM] * 2,
        [field, field, (shape((ranks, WIDE), BF16), VMEM), (shape(coef, BF16), VMEM)],
        [
            pltpu.VMEM(vectors.shape, BF16),
            pltpu.VMEM(bases.shape, BF16),
            pltpu.VMEM((2 * rows, LANES), F32),
            pltpu.SemaphoreType.DMA((2,)),
        ],
        8,
    )


def first_near(
    slabs, peers, near_count, near_src, near_type, far_src, tiles, coupling, lo, hi, chip, further
):
    blocks, partners, _ = coupling.shape
    rows, rim = blocks * RHS, RIM * RHS
    types = tiles.shape[0]
    table = (TILE, types * WIDE)
    slots = (near_src.shape, jnp.int32)
    picks = (far_src.shape, jnp.int32)
    return call(
        functools.partial(first_near_kernel, slabs, blocks * peers), "first_near",
        (near_count, near_src, near_type, far_src, tiles, coupling, lo, hi, chip, further),
        [HBM] * 6 + [VMEM] * 4,
        [
            (shape((rows, WIDE), F32), VMEM),
            (shape((blocks * RANK, partners * RANK), BF16), VMEM),
            (shape(table, BF16), HBM),
            (shape(*picks), SMEM),
            (shape(*slots), SMEM),
            (shape(*slots), SMEM),
        ],
        [
            pltpu.SMEM(near_count.shape, jnp.int32),
            pltpu.VMEM(*slots),
            pltpu.VMEM(*slots),
            pltpu.VMEM(*picks),
            pltpu.VMEM(tiles.shape, BF16),
            pltpu.VMEM(coupling.shape, BF16),
            pltpu.VMEM(*picks),
            pltpu.VMEM(*slots),
            pltpu.VMEM(*slots),
            pltpu.VMEM((2 * rim, LANES), F32),
            pltpu.VMEM((4 * rim, WIDE), BF16),
            pltpu.VMEM((rows, (types + 1) * WIDE), BF16),
            pltpu.VMEM(table, BF16),
            pltpu.SemaphoreType.DMA((9 + STEPS,)),
        ],
        20, LONG,
    )


def give(lo, hi, table):
    rows = 2 * lo.shape[0]
    y = (rows // RHS, RHS * TILE)
    return call(
        give_kernel, "give", (lo, hi, table), [VMEM] * 2 + [HBM],
        [(shape(y, BF16), HBM), (shape(table.shape, BF16), KEPT)],
        [
            pltpu.VMEM((2 * rows, LANES), F32),
            pltpu.VMEM(y, BF16),
            pltpu.SemaphoreType.DMA((2,)),
        ],
        4, 12_000_000,
    )


def second_near(at, kind, lo, hi, chip, further, table):
    rows = 2 * lo.shape[0]
    return call(
        second_near_kernel, "second_near", (at, kind, lo, hi, further, chip, table),
        [SMEM] * 2 + [VMEM] * 4 + [KEPT],
        [(shape((rows, WIDE), F32), VMEM)],
        [
            pltpu.VMEM((2 * rows, WIDE), BF16),
            pltpu.VMEM((rows, table.shape[1] + WIDE), BF16),
        ],
        8, 12_000_000,
    )[0]


def far(last, idx, got, mat, basis, near_term):
    rows = near_term.shape[0]
    peers, packed, _ = got.shape
    scratch = [
        pltpu.VMEM((SIDE * peers * packed, LANES), BF16),
        pltpu.VMEM((rows, mat.shape[1]), BF16),
    ]
    if last:
        outs = [(shape((rows // RHS, RHS * TILE), BF16), VMEM)]
        scratch.append(pltpu.VMEM((2 * rows, LANES), F32))
    else:
        outs = [(shape((rows // 2, WIDE), BF16), VMEM)] * 4 + [(shape(got.shape, BF16), VMEM)]
    return call(
        functools.partial(far_kernel, last), "far_last" if last else "far",
        (idx, got, mat, basis, near_term), [SMEM] + [VMEM] * 4, outs, scratch, 8,
    )


def per_device(vectors, tiles, near_src, near_type, near_count, bases, far_src, coupling):
    slabs, peers = lax.axis_size("slab"), lax.axis_size("grp")
    chips = [(i, i ^ 1) for i in range(slabs)]
    between = [(i, (i + 1 if i % 2 else i - 1) % slabs) for i in range(slabs)]

    def halo(chip, further):
        return lax.ppermute(chip, "slab", chips), lax.ppermute(further, "slab", between)

    def exchange(coef):
        return lax.all_to_all(coef, "grp", 0, 0, tiled=True)

    chip, further = halo(vectors, vectors)
    lo, hi, basis, coef = opening(peers, vectors, bases)
    got = exchange(coef)
    near_term, mat, table, idx, at, kind = first_near(
        slabs, peers, near_count, near_src, near_type, far_src, tiles, coupling, lo, hi, chip, further
    )
    lo, hi, chip, further, coef = far(False, idx, got, mat, basis, near_term)
    got = exchange(coef)
    chip, further = halo(chip, further)
    first, table = give(lo, hi, table)
    near_term = second_near(at, kind, lo, hi, chip, further, table)
    (second,) = far(True, idx, got, mat, basis, near_term)
    return (first, second)


def solution(mesh):
    in_specs = (
        P(("slab", "grp"), None),
        P(),
        P(("slab", "grp"), None),
        P(("slab", "grp"), None),
        P(("slab", "grp")),
        P(("slab", "grp"), None),
        P(("slab", "grp"), None),
        P(("slab", "grp"), None, None),
    )
    out_specs = (P(("slab", "grp"), None), P(("slab", "grp"), None))
    return jax.shard_map(
        per_device, mesh=mesh, in_specs=in_specs, out_specs=out_specs, check_vma=False
    )
```
